32 devices in a mesh: seq: 16 (over z, x, core), wt: 2 (over y).
Axes of the slice: x: 2, y: 2, z: 4, core: 2. Of those that a mesh axis runs over, the one named last changes fastest.
Arguments:
- tokens: int32 [2, 2048], P('wt', 'seq'), may hold values from 0 to 511
- embed_table: bfloat16 [512, 8192], P(None, 'wt'), may hold values from -8 to 8
- norm_gain: bfloat16 [8192], P('wt'), may hold values from 0.099609375 to 1.8984375
- w_in: bfloat16 [8192, 3, 4096], P('wt', None, 'seq'), may hold values from -0.0625 to 0.0625
- short_taps: bfloat16 [3, 3, 4096], P(None, None, 'seq'), may hold values from -3 to 3
- filters: bfloat16 [256, 128], P('seq'), may hold values from -2 to 2
- w_out: bfloat16 [8192, 4096], P('wt'), may hold values from -0.09375 to 0.09375
Outputs:
- block_out: bfloat16 [2, 2048, 8192], P(None, 'seq', 'wt')
The draws below stay inside these ranges and needn't reach their ends.
All inputs are finite; a program needn't handle non-finite values.
Results may differ from the reference program's by a relative error of at most 0.0088.
Values may be sent and summed in bfloat16 or wider, within the bound.
No kernel may reach another device: no remote copies, remote signals or barrier semaphores. Data moves between devices by JAX's collectives and lax.ppermute only.
A program may use at most 128 MiB of HBM per device.

```python
import math
import jax
import jax.numpy as jnp
import numpy as np
from jax import lax

D = 8192
V = 512
GSZ = 16
FILT = 128
C = 4096
GRP = 256
SEQS = 2
L = 2048


def draw_embed_table(key, part):
    key_base = jax.random.fold_in(key, 21)
    key_cols = jax.random.fold_in(key, 22)
    key_rows = jax.random.fold_in(key, 23)
    feature_pos = jnp.arange(D).astype(jnp.float32) / D
    col_scale = 0.35 * jnp.exp(math.log(3.0) * feature_pos) * jnp.exp(jax.random.uniform(key_cols, (D,), jnp.float32, -0.3, 0.3))
    base_vals = jnp.clip(jax.random.normal(key_base, (V, D), jnp.float32), -3.0, 3.0)
    row_scale = jnp.exp(jax.random.uniform(key_rows, (V, 1), jnp.float32, math.log(0.6), math.log(1.6)))
    return (base_vals * row_scale * col_scale[None, :]).astype(jnp.bfloat16)


def draw_filters(key, part):
    key_rate = jax.random.fold_in(key, 11)
    key_vals = jax.random.fold_in(key, 12)
    log_rate = jax.random.uniform(key_rate, (GRP, 1), jnp.float32, math.log(1.0 / 3000.0), math.log(1.0 / 8.0))
    values = jnp.clip(jax.random.normal(key_vals, (GRP, FILT), jnp.float32), -4.0, 4.0)
    rate = jnp.exp(log_rate)
    positions = jnp.arange(FILT).astype(jnp.float32)[None, :]
    scale = jnp.sqrt(jnp.maximum(2.0 * rate, 1.0 / FILT))
    return (values * jnp.exp(-rate * positions) * scale).astype(jnp.bfloat16)


def plant(array, stream_key, smallest, high):
    shape = array.shape
    place = [jax.random.randint(jax.random.fold_in(stream_key, axis), (), 0, shape[axis]) for axis in range(len(shape))]
    array = array.at[tuple(place)].set(smallest)
    longest = shape.index(max(shape))
    place[longest] = (place[longest] + 1) % shape[longest]
    return array.at[tuple(place)].set(high)


def block_levels(own_key, shape, cuts, least, largest):
    loudness = 1.0
    for position, parts in cuts:
        heights = jax.random.uniform(jax.random.fold_in(jax.random.fold_in(own_key, 6), position), (parts,), jnp.float32, least / len(cuts), largest / len(cuts))
        loudness = loudness * jnp.repeat(jnp.exp(heights), shape[position] // parts).reshape((-1,) + (1,) * (len(shape) - 1 - position))
    return loudness


def rank_table(number_of, slope):
    weights = [(1 << 20) // math.isqrt(standing ** slope) + 1 for standing in range(1, number_of + 1)]
    scale = 1 + sum(weights) // (1 << 30)
    return np.cumsum(np.array([max(1, weight // scale) for weight in weights]))


def ranked(own_key, dims, count, skew):
    grid = rank_table(count, skew)
    ticket = jax.random.randint(jax.random.fold_in(own_key, 1), dims, 0, int(grid[count - 1]))
    grade = jnp.searchsorted(jnp.asarray(grid, jnp.int32), ticket, side="right")
    return jax.random.permutation(jax.random.fold_in(own_key, 2), count)[grade].astype(jnp.int32)


def scatter_about(stream_key, extent, deviation, reach, split=(), held_as=jnp.bfloat16):
    result = jax.random.normal(stream_key, extent, jnp.float32) * deviation
    if len(split) > 0:
        result = block_levels(stream_key, extent, split, -0.22, 0.18) * result
    return jnp.clip(result, min=-reach, max=reach).astype(held_as)


def setup_inputs(seed: int = 0) -> dict:
    splits = jax.random.split(jax.random.key(seed), 8)
    tokens = plant(ranked(splits[0], (SEQS, L), V, 2), jax.random.fold_in(splits[0], 3), 0, V - 1).astype(jnp.int32)
    embed_table = draw_embed_table(jax.random.fold_in(splits[7], 71), 0)
    norm_gain = jnp.clip(1.0 + 0.18 * jax.random.normal(splits[2], (D,), jnp.float32), 0.099609375, 1.8984375).astype(jnp.bfloat16)
    w_in = scatter_about(splits[3], (D, 3, C), D ** -0.5, 0.0625, ((0, 2), (2, 16)))
    short_taps = scatter_about(splits[4], (3, 3, C), 0.6, 3.0, ((2, 16),))
    filters = draw_filters(jax.random.fold_in(splits[7], 71), 0)
    w_out = scatter_about(splits[6], (D, C), C ** -0.5, 0.09375, ((0, 2),))
    return dict(tokens=tokens, embed_table=embed_table, norm_gain=norm_gain, w_in=w_in, short_taps=short_taps, filters=filters, w_out=w_out)


def causal_pair(filter_vals):
    tap_count = filter_vals.shape[1]
    group_count = filter_vals.shape[0]
    tiled_taps = jnp.tile(filter_vals, (1, 2 * tap_count - 1)).reshape(group_count, tap_count, 2 * tap_count - 1)[:, :, :tap_count]
    circulant = jnp.swapaxes(tiled_taps, 1, 2)
    row_pos = lax.broadcasted_iota(jnp.int32, (tap_count, tap_count), 0)
    col_pos = lax.broadcasted_iota(jnp.int32, (tap_count, tap_count), 1)
    lower_mask = (row_pos >= col_pos)[None]
    zero_mat = jnp.zeros_like(circulant)
    return (jnp.where(lower_mask, circulant, zero_mat), jnp.where(lower_mask, zero_mat, circulant))

def reference(tokens, embed_table, norm_gain, w_in, short_taps, filters, w_out):
    table_vals = embed_table.astype(jnp.float32)
    row_scale = lax.rsqrt(lax.optimization_barrier(jnp.mean(table_vals * table_vals, axis=1, keepdims=True)) + 1e-06)
    normed = (table_vals * row_scale * norm_gain.astype(jnp.float32)).astype(jnp.bfloat16)
    vocab_flat = jnp.dot(normed, w_in.reshape(D, 3 * C), preferred_element_type=jnp.float32).astype(jnp.bfloat16)
    vocab_proj = vocab_flat.reshape(V, 3, C)
    tap_vals = short_taps.astype(jnp.float32)
    lower_mat, upper_mat = causal_pair(filters.astype(jnp.float32))

    def one_genome(token_ids):
        embedded = jnp.take(embed_table, token_ids, axis=0)
        projected = jnp.take(vocab_proj, token_ids, axis=0)
        extended = jnp.concatenate([jnp.zeros((2, 3, C), jnp.bfloat16), projected], axis=0).astype(jnp.float32)
        mixture = tap_vals[0] * extended[2:] + tap_vals[1] * extended[1:-1] + tap_vals[2] * extended[:-2]
        product = lax.optimization_barrier((mixture[:, 0] * mixture[:, 2]).astype(jnp.bfloat16)).astype(jnp.float32)
        padded = jnp.concatenate([jnp.zeros((FILT, C), jnp.float32), product], axis=0)
        stacked = padded.reshape(L // FILT + 1, FILT, GRP, GSZ)
        filtered = jnp.einsum('gij,bjgc->bigc', lower_mat, stacked[1:], precision=lax.Precision.HIGHEST)
        filtered = filtered + jnp.einsum('gij,bjgc->bigc', upper_mat, stacked[:-1], precision=lax.Precision.HIGHEST)
        filtered = filtered.reshape(L, C)
        gated = (mixture[:, 1] * filtered).astype(jnp.bfloat16)
        branch = jnp.dot(gated, w_out.T, preferred_element_type=jnp.float32)
        return (embedded.astype(jnp.float32) + branch).astype(jnp.bfloat16)
    return lax.map(one_genome, tokens)
```

```python
import functools

import jax
import jax.numpy as jnp
from jax import lax
from jax.experimental import pallas as pl
from jax.experimental.pallas import tpu as pltpu
from jax.sharding import PartitionSpec as P

LANES = 128
MIB = 1 << 20


def shifted(shard, axis, by):
    size = lax.axis_size(axis)
    pairs = [(i, i + by) for i in range(size) if 0 <= i + by < size]
    return lax.ppermute(shard, axis, pairs)


def causal_pair(filter_vals):
    tap_count = filter_vals.shape[1]
    group_count = filter_vals.shape[0]
    tiled_taps = jnp.tile(filter_vals, (1, 2 * tap_count - 1)).reshape(
        group_count, tap_count, 2 * tap_count - 1
    )[:, :, :tap_count]
    circulant = jnp.swapaxes(tiled_taps, 1, 2)
    row_pos = lax.broadcasted_iota(jnp.int32, (tap_count, tap_count), 0)
    col_pos = lax.broadcasted_iota(jnp.int32, (tap_count, tap_count), 1)
    lower_mask = (row_pos >= col_pos)[None]
    zero_mat = jnp.zeros_like(circulant)
    return (jnp.where(lower_mask, circulant, zero_mat), jnp.where(lower_mask, zero_mat, circulant))


def short_mix(extended, tap_vals):
    row_count = extended.shape[0] - 2
    ext_vals = extended.astype(jnp.float32)
    return (
        tap_vals[0] * ext_vals[2 : 2 + row_count]
        + tap_vals[1] * ext_vals[1 : 1 + row_count]
        + tap_vals[2] * ext_vals[0:row_count]
    )


def run_filter(extended, lower_mat, upper_mat):
    tap_count = lower_mat.shape[1]
    group_count = lower_mat.shape[0]
    chan_count = extended.shape[1]
    blocks = extended.shape[0] // tap_count
    stacked = extended.reshape(blocks, tap_count, group_count, chan_count // group_count)
    filtered = jnp.einsum(
        "gij,bjgc->bigc", lower_mat, stacked[1:], preferred_element_type=jnp.float32
    )
    filtered = filtered + jnp.einsum(
        "gij,bjgc->bigc", upper_mat, stacked[:-1], preferred_element_type=jnp.float32
    )
    return filtered.reshape((blocks - 1) * tap_count, chan_count)


def plain_block(tokens, embed_table, norm_gain, w_in, short_taps, filters, w_out):
    token_ids = tokens[0]
    own_len = token_ids.shape[0]
    tap_count = filters.shape[1]
    table_vals = embed_table.astype(jnp.float32)
    square_sums = lax.psum(jnp.sum(table_vals * table_vals, axis=1, keepdims=True), "wt")
    feature_count = embed_table.shape[1] * lax.axis_size("wt")
    row_scale = lax.rsqrt(square_sums / feature_count + 1e-06)
    normed = (table_vals * row_scale * norm_gain.astype(jnp.float32)).astype(jnp.bfloat16)
    local_chans = w_in.shape[2]
    w_flat = w_in.reshape(w_in.shape[0], 3 * local_chans)
    vocab_size = embed_table.shape[0]
    partial_sum = jnp.dot(normed, w_flat, preferred_element_type=jnp.float32)
    vocab_flat = lax.psum(partial_sum, "wt").astype(jnp.bfloat16)
    vocab_proj = vocab_flat.reshape(vocab_size, 3, local_chans)
    vocab_all, tap_all, filter_all = (
        lax.all_gather(vocab_proj, "seq", axis=2, tiled=True),
        lax.all_gather(short_taps, "seq", axis=2, tiled=True),
        lax.all_gather(filters, "seq", axis=0, tiled=True),
    )
    projected = jnp.take(vocab_all, token_ids, axis=0)
    edge_prev = shifted(projected[own_len - 2 :], "seq", 1)
    mixture = short_mix(
        jnp.concatenate([edge_prev, projected], axis=0), tap_all.astype(jnp.float32)
    )
    product = (mixture[:, 0] * mixture[:, 2]).astype(jnp.bfloat16)
    tail_prev = shifted(product[own_len - tap_count + 1 :], "seq", 1)
    chan_count = product.shape[1]
    extended = jnp.concatenate(
        [jnp.zeros((1, chan_count), jnp.bfloat16), tail_prev, product], axis=0
    )
    lower_mat, upper_mat = causal_pair(filter_all)
    filtered = run_filter(extended, lower_mat, upper_mat)
    gated = (mixture[:, 1] * filtered).astype(jnp.bfloat16)
    everyone = lax.all_gather(tokens, "wt", axis=0, tiled=True)
    branch = jnp.einsum(
        "knc,dc->knd",
        lax.all_gather(gated[None], "wt", axis=0, tiled=True),
        w_out,
        preferred_element_type=jnp.float32,
    )
    embedded = jnp.take(embed_table, everyone, axis=0)
    return (embedded.astype(jnp.float32) + branch).astype(jnp.bfloat16)


def vocab_share_body(half_ref, emb_ref, gain_ref, w_ref, out_ref, *rest, steps, squares):
    if squares:
        sq_ref, acc_ref, sq_acc = rest
    else:
        (acc_ref,) = rest
    step = pl.program_id(0)
    emb = emb_ref[...]
    scaled = emb * gain_ref[...]
    weights = jnp.concatenate([w_ref[s] for s in range(w_ref.shape[0])], axis=1)
    term = jnp.dot(scaled, weights, preferred_element_type=jnp.float32)
    if squares:
        vals = emb.astype(jnp.float32)
        vals = vals * vals
        part = vals[:, :LANES]
        for i in range(1, vals.shape[1] // LANES):
            part = part + vals[:, i * LANES : (i + 1) * LANES]

    @pl.when(step == 0)
    def _():
        acc_ref[...] = term
        if squares:
            sq_acc[...] = part

    @pl.when(step > 0)
    def _():
        acc_ref[...] += term
        if squares:
            sq_acc[...] += part

    @pl.when(step == steps - 1)
    def _():
        out_ref[...] = acc_ref[...].astype(out_ref.dtype)
        if squares:
            sq_ref[...] = jnp.sum(sq_acc[...].T, axis=0, keepdims=True)


def vocab_share(half, embed_table, gain_row, w_streams, out_dtype, squares):
    vocab, feats = embed_table.shape
    streams, _, local_chans = w_streams.shape
    chans = local_chans // 2
    depth = feats // 4 if feats % (4 * LANES) == 0 else feats
    steps = feats // depth
    width = streams * chans
    out_shape = [jax.ShapeDtypeStruct((vocab, width), out_dtype)]
    out_specs = [pl.BlockSpec((vocab, width), lambda k, h: (0, 0))]
    scratch = [pltpu.VMEM((vocab, width), jnp.float32)]
    if squares:
        out_shape.append(jax.ShapeDtypeStruct((1, vocab), jnp.float32))
        out_specs.append(pl.BlockSpec((1, vocab), lambda k, h: (0, 0)))
        scratch.append(pltpu.VMEM((vocab, LANES), jnp.float32))
    return pl.pallas_call(
        functools.partial(vocab_share_body, steps=steps, squares=squares),
        grid_spec=pltpu.PrefetchScalarGridSpec(
            num_scalar_prefetch=1,
            grid=(steps,),
            in_specs=[
                pl.BlockSpec((vocab, depth), lambda k, h: (0, k)),
                pl.BlockSpec((1, depth), lambda k, h: (0, k)),
                pl.BlockSpec((streams, depth, chans), lambda k, h: (0, k, h[0])),
            ],
            out_specs=out_specs,
            scratch_shapes=scratch,
        ),
        out_shape=out_shape,
        compiler_params=pltpu.CompilerParams(vmem_limit_bytes=40 * MIB),
        cost_estimate=pl.CostEstimate(
            flops=2 * vocab * feats * width,
            bytes_accessed=2 * feats * (vocab + width),
            transcendentals=0,
        ),
        name="vocab_share",
    )(half, embed_table, gain_row, w_streams)


def mixer_body(
    place_ref, tok_ref, own_ref, got_ref, sq_ref, sq_got_ref, taps_ref, filt_ref, out_ref,
    vocab_t, toeplitz, tap_cols, carry, prod, gate, conv, *, feature_count, chunk,
):
    chans = out_ref.shape[-1]
    vocab = vocab_t.shape[1]
    length = tok_ref.shape[-1]
    groups = filt_ref.shape[0]
    taps = filt_ref.shape[1]
    gsz = chans // groups
    blocks = length // taps

    @pl.when(pl.program_id(0) == 0)
    def _():
        sums = (own_ref[...] + got_ref[...].astype(jnp.float32)).T
        scale = lax.rsqrt((sq_ref[...] + sq_got_ref[...]) / feature_count + 1e-06)
        vocab_t[...] = (sums * scale).astype(jnp.bfloat16)
        row = lax.broadcasted_iota(jnp.int32, (taps, taps), 0)
        col = lax.broadcasted_iota(jnp.int32, (taps, taps), 1)
        filt = filt_ref[...].astype(jnp.float32)
        for g in range(groups):
            circ = pltpu.roll(
                jnp.broadcast_to(filt[g : g + 1], (taps, taps)), 0, 1, stride=1, stride_axis=0
            )
            toeplitz[g, :taps] = jnp.where(col < row, circ, 0.0).astype(jnp.bfloat16)
            toeplitz[g, taps:] = jnp.where(col >= row, circ, 0.0).astype(jnp.bfloat16)
        tap_cols[...] = taps_ref[...].T
        prod[:, :gsz, :] = jnp.zeros((groups, gsz, taps), jnp.bfloat16)

    for k in range(2):
        carry[k] = jnp.zeros(carry.shape[1:], jnp.float32)

    ids = lax.broadcasted_iota(jnp.int32, (vocab, chunk), 0)
    lane = lax.broadcasted_iota(jnp.int32, (chans, LANES), 1)
    for n in range(length // chunk):
        picks = jnp.where(ids == tok_ref[0, :, n * chunk : (n + 1) * chunk], 1.0, 0.0)
        proj = jnp.dot(vocab_t[...], picks.astype(jnp.bfloat16), preferred_element_type=jnp.float32)
        mixed = []
        for s in range(3):
            cur = proj[s * chans : (s + 1) * chans]
            total = tap_cols[:, s : s + 1] * cur
            for k in (1, 2):
                back = pltpu.roll(cur, k, 1)
                head = jnp.where(lane < k, carry[k - 1, s], back[:, :LANES])
                carry[k - 1, s] = back[:, :LANES]
                back = jnp.concatenate([head, back[:, LANES:]], axis=1)
                total = total + tap_cols[:, 3 * k + s : 3 * k + s + 1] * back
            mixed.append(total)
        gate[:, n * chunk : (n + 1) * chunk] = mixed[1]
        inner = (mixed[0] * mixed[2]).astype(jnp.bfloat16)
        for b in range(chunk // taps):
            at = (n * (chunk // taps) + b + 1) * gsz
            for g in range(groups):
                prod[g, at : at + gsz, :] = inner[g * gsz : (g + 1) * gsz, b * taps : (b + 1) * taps]
    rows = blocks * gsz
    for g in range(groups):
        pair = jnp.concatenate([prod[g, :rows], prod[g, gsz : gsz + rows]], axis=1)
        conv[g] = jnp.dot(pair, toeplitz[g], preferred_element_type=jnp.float32)
    for b in range(blocks):
        filtered = jnp.concatenate(
            [conv[g, b * gsz : (b + 1) * gsz, :] for g in range(groups)], axis=0
        )
        gated = gate[:, b * taps : (b + 1) * taps] * filtered
        out_ref[b, 0] = gated.T.astype(jnp.bfloat16)


def mixer(place, tokens, own, got, squares, squares_got, taps_rows, filt, feature_count):
    genomes, length = tokens.shape
    vocab, width = own.shape
    chans = width // 3
    groups, taps = filt.shape
    gsz = chans // groups
    blocks = length // taps
    chunk = 2 * taps
    whole = lambda *shape: pl.BlockSpec(shape, lambda g, p: (0,) * len(shape))
    return pl.pallas_call(
        functools.partial(mixer_body, feature_count=feature_count, chunk=chunk),
        grid_spec=pltpu.PrefetchScalarGridSpec(
            num_scalar_prefetch=1,
            grid=(genomes,),
            in_specs=[
                pl.BlockSpec((1, 1, length), lambda g, p: (g, 0, 0)),
                whole(vocab, width),
                whole(vocab, width),
                whole(1, vocab),
                whole(1, vocab),
                whole(*taps_rows.shape),
                whole(groups, taps),
            ],
            out_specs=pl.BlockSpec((blocks, 1, taps, chans), lambda g, p: (0, g, 0, 0)),
            scratch_shapes=[
                pltpu.VMEM((width, vocab), jnp.bfloat16),
                pltpu.VMEM((groups, 2 * taps, taps), jnp.bfloat16),
                pltpu.VMEM((chans, taps_rows.shape[0]), jnp.float32),
                pltpu.VMEM((2, 3, chans, LANES), jnp.float32),
                pltpu.VMEM((groups, (blocks + 1) * gsz, taps), jnp.bfloat16),
                pltpu.VMEM((chans, length), jnp.float32),
                pltpu.VMEM((groups, blocks * gsz, taps), jnp.float32),
            ],
        ),
        out_shape=jax.ShapeDtypeStruct((blocks, genomes, taps, chans), jnp.bfloat16),
        compiler_params=pltpu.CompilerParams(vmem_limit_bytes=40 * MIB),
        cost_estimate=pl.CostEstimate(
            flops=2 * genomes * length * vocab * width,
            bytes_accessed=6 * vocab * width + 2 * genomes * length * chans,
            transcendentals=0,
        ),
        name="mixer",
    )(place, tokens[:, None, :], own, got, squares, squares_got, taps_rows, filt)


def project_body(tok_ref, mine_ref, other_ref, table_ref, w_ref, out_ref, gated, picks, *, which):
    sources, genomes, rows, chans = mine_ref.shape

    @pl.when(pl.program_id(0) == 0)
    def _():
        vocab = table_ref.shape[0]
        ids = lax.broadcasted_iota(jnp.int32, (vocab, genomes * rows), 0)
        hot = jnp.where(ids == tok_ref[...], 1.0, 0.0)
        picks[...] = hot.T.astype(jnp.bfloat16)
        me = lax.axis_index("wt")
        for ref, at in ((mine_ref, me), (other_ref, 1 - me)):
            for s in range(sources):
                lanes = pl.ds(pl.multiple_of((2 * s + at) * chans, LANES), chans)
                for g in range(genomes):
                    gated[g * rows : (g + 1) * rows, lanes] = ref[s, g]

    total = lax.dot_general(
        gated[...], w_ref[...], (((1,), (1,)), ((), ())), preferred_element_type=jnp.float32
    )
    total = total + jnp.dot(picks[...], table_ref[...], preferred_element_type=jnp.float32)
    for g in range(genomes):
        out_ref[g] = total[g * rows : (g + 1) * rows].astype(jnp.bfloat16)


def project(tok_row, mine, other, embed_table, w_out):
    sources, genomes, rows, chans = mine.shape
    feats, depth = w_out.shape
    vocab = embed_table.shape[0]
    tile = 512
    whole = lambda *shape: pl.BlockSpec(shape, lambda f: (0,) * len(shape))
    return pl.pallas_call(
        functools.partial(project_body, which=None),
        grid=(feats // tile,),
        in_specs=[
            whole(1, genomes * rows),
            whole(*mine.shape),
            whole(*mine.shape),
            pl.BlockSpec((vocab, tile), lambda f: (0, f)),
            pl.BlockSpec((tile, depth), lambda f: (f, 0)),
        ],
        out_specs=pl.BlockSpec((genomes, rows, tile), lambda f: (0, 0, f)),
        scratch_shapes=[
            pltpu.VMEM((genomes * rows, depth), jnp.bfloat16),
            pltpu.VMEM((genomes * rows, vocab), jnp.bfloat16),
        ],
        out_shape=jax.ShapeDtypeStruct((genomes, rows, feats), jnp.bfloat16),
        compiler_params=pltpu.CompilerParams(vmem_limit_bytes=40 * MIB),
        cost_estimate=pl.CostEstimate(
            flops=2 * genomes * rows * feats * (depth + vocab),
            bytes_accessed=2 * feats * (depth + vocab + genomes * rows),
            transcendentals=0,
        ),
        name="project",
    )(tok_row, mine, other, embed_table, w_out)


def swap_wt(shard):
    return lax.ppermute(shard, "wt", [(0, 1), (1, 0)])


def shared_block(tokens, embed_table, norm_gain, w_in, short_taps, filters, w_out):
    me = lax.axis_index("wt")
    local_chans = w_in.shape[2]
    chans = local_chans // 2
    groups = filters.shape[0] // 2
    feature_count = embed_table.shape[1] * lax.axis_size("wt")
    w_streams = jnp.transpose(w_in, (1, 0, 2))
    gain_row = norm_gain[None]
    pick = lambda which: jnp.reshape(which, (1,)).astype(jnp.int32)
    sent, squares = vocab_share(pick(1 - me), embed_table, gain_row, w_streams, jnp.bfloat16, True)
    got = swap_wt(sent)
    squares_got = swap_wt(squares)
    (own,) = vocab_share(pick(me), embed_table, gain_row, w_streams, jnp.float32, False)
    other_tokens = swap_wt(tokens)
    both = jnp.where(
        me == 0,
        jnp.concatenate([tokens, other_tokens], axis=0),
        jnp.concatenate([other_tokens, tokens], axis=0),
    )
    all_tokens = lax.all_gather(both, "seq", axis=1, tiled=True)
    taps_rows = lax.dynamic_slice_in_dim(
        short_taps.astype(jnp.float32).reshape(9, local_chans), me * chans, chans, 1
    )
    taps_rows = jnp.pad(taps_rows, ((0, 7), (0, 0)))
    filt = lax.dynamic_slice_in_dim(filters, me * groups, groups, 0)
    gated = mixer(pick(me), all_tokens, own, got, squares, squares_got, taps_rows, filt, feature_count)
    mine = lax.all_to_all(gated, "seq", 0, 0, tiled=True)
    other = swap_wt(mine)
    return project(both.reshape(1, -1), mine, other, embed_table, w_out)


def local(*args):
    tokens, embed_table, norm_gain, w_in, short_taps, filters, w_out = args
    wide = lax.axis_size("wt") == 2 and w_in.shape[2] % (2 * LANES) == 0
    aligned = tokens.shape[1] == filters.shape[1] == LANES and w_out.shape[0] % 512 == 0
    if wide and aligned and w_in.shape[2] == 2 * LANES:
        return shared_block(*args)
    return plain_block(*args)


def solution(mesh):
    placed = (
        P("wt", "seq"),
        P(None, "wt"),
        P("wt"),
        P("wt", None, "seq"),
        P(None, None, "seq"),
        P("seq", None),
        P("wt", None),
    )
    return jax.shard_map(
        local, mesh=mesh, in_specs=placed, out_specs=P(None, "seq", "wt"), check_vma=False
    )
```

```python
import functools

import jax
import jax.numpy as jnp
from jax import lax
from jax.experimental import pallas as pl
from jax.experimental.pallas import tpu as pltpu
from jax.sharding import PartitionSpec as P

LANES = 128
MIB = 1 << 20


def shifted(shard, axis, by):
    size = lax.axis_size(axis)
    pairs = [(i, i + by) for i in range(size) if 0 <= i + by < size]
    return lax.ppermute(shard, axis, pairs)


def causal_pair(filter_vals):
    tap_count = filter_vals.shape[1]
    group_count = filter_vals.shape[0]
    tiled_taps = jnp.tile(filter_vals, (1, 2 * tap_count - 1)).reshape(
        group_count, tap_count, 2 * tap_count - 1
    )[:, :, :tap_count]
    circulant = jnp.swapaxes(tiled_taps, 1, 2)
    row_pos = lax.broadcasted_iota(jnp.int32, (tap_count, tap_count), 0)
    col_pos = lax.broadcasted_iota(jnp.int32, (tap_count, tap_count), 1)
    lower_mask = (row_pos >= col_pos)[None]
    zero_mat = jnp.zeros_like(circulant)
    return (jnp.where(lower_mask, circulant, zero_mat), jnp.where(lower_mask, zero_mat, circulant))


def short_mix(extended, tap_vals):
    row_count = extended.shape[0] - 2
    ext_vals = extended.astype(jnp.float32)
    return (
        tap_vals[0] * ext_vals[2 : 2 + row_count]
        + tap_vals[1] * ext_vals[1 : 1 + row_count]
        + tap_vals[2] * ext_vals[0:row_count]
    )


def run_filter(extended, lower_mat, upper_mat):
    tap_count = lower_mat.shape[1]
    group_count = lower_mat.shape[0]
    chan_count = extended.shape[1]
    blocks = extended.shape[0] // tap_count
    stacked = extended.reshape(blocks, tap_count, group_count, chan_count // group_count)
    filtered = jnp.einsum(
        "gij,bjgc->bigc", lower_mat, stacked[1:], preferred_element_type=jnp.float32
    )
    filtered = filtered + jnp.einsum(
        "gij,bjgc->bigc", upper_mat, stacked[:-1], preferred_element_type=jnp.float32
    )
    return filtered.reshape((blocks - 1) * tap_count, chan_count)


def plain_block(tokens, embed_table, norm_gain, w_in, short_taps, filters, w_out):
    token_ids = tokens[0]
    own_len = token_ids.shape[0]
    tap_count = filters.shape[1]
    table_vals = embed_table.astype(jnp.float32)
    square_sums = lax.psum(jnp.sum(table_vals * table_vals, axis=1, keepdims=True), "wt")
    feature_count = embed_table.shape[1] * lax.axis_size("wt")
    row_scale = lax.rsqrt(square_sums / feature_count + 1e-06)
    normed = (table_vals * row_scale * norm_gain.astype(jnp.float32)).astype(jnp.bfloat16)
    local_chans = w_in.shape[2]
    w_flat = w_in.reshape(w_in.shape[0], 3 * local_chans)
    vocab_size = embed_table.shape[0]
    partial_sum = jnp.dot(normed, w_flat, preferred_element_type=jnp.float32)
    vocab_flat = lax.psum(partial_sum, "wt").astype(jnp.bfloat16)
    vocab_proj = vocab_flat.reshape(vocab_size, 3, local_chans)
    vocab_all, tap_all, filter_all = (
        lax.all_gather(vocab_proj, "seq", axis=2, tiled=True),
        lax.all_gather(short_taps, "seq", axis=2, tiled=True),
        lax.all_gather(filters, "seq", axis=0, tiled=True),
    )
    projected = jnp.take(vocab_all, token_ids, axis=0)
    edge_prev = shifted(projected[own_len - 2 :], "seq", 1)
    mixture = short_mix(
        jnp.concatenate([edge_prev, projected], axis=0), tap_all.astype(jnp.float32)
    )
    product = (mixture[:, 0] * mixture[:, 2]).astype(jnp.bfloat16)
    tail_prev = shifted(product[own_len - tap_count + 1 :], "seq", 1)
    chan_count = product.shape[1]
    extended = jnp.concatenate(
        [jnp.zeros((1, chan_count), jnp.bfloat16), tail_prev, product], axis=0
    )
    lower_mat, upper_mat = causal_pair(filter_all)
    filtered = run_filter(extended, lower_mat, upper_mat)
    gated = (mixture[:, 1] * filtered).astype(jnp.bfloat16)
    everyone = lax.all_gather(tokens, "wt", axis=0, tiled=True)
    branch = jnp.einsum(
        "knc,dc->knd",
        lax.all_gather(gated[None], "wt", axis=0, tiled=True),
        w_out,
        preferred_element_type=jnp.float32,
    )
    embedded = jnp.take(embed_table, everyone, axis=0)
    return (embedded.astype(jnp.float32) + branch).astype(jnp.bfloat16)


def vocab_share_body(half_ref, gain_ref, *refs, slabs, steps, squares):
    embs, weights = refs[:slabs], refs[slabs : 2 * slabs]
    out_ref = refs[2 * slabs]
    if squares:
        sq_ref, acc_ref, sq_acc = refs[2 * slabs + 1 :]
    else:
        acc_ref = refs[2 * slabs + 1]
    step = pl.program_id(0)
    depth = embs[0].shape[1]
    term = part = None
    for j in range(slabs):
        emb = embs[j][...]
        at = pl.multiple_of((step * slabs + j) * depth, LANES)
        scaled = emb * gain_ref[pl.ds(at, depth)][None]
        wide = jnp.concatenate([weights[j][s] for s in range(weights[j].shape[0])], axis=1)
        more = jnp.dot(scaled, wide, preferred_element_type=jnp.float32)
        term = more if term is None else term + more
        if squares:
            vals = emb.astype(jnp.float32)
            vals = vals * vals
            for i in range(depth // LANES):
                piece = vals[:, i * LANES : (i + 1) * LANES]
                part = piece if part is None else part + piece

    @pl.when(step == 0)
    def _():
        acc_ref[...] = term
        if squares:
            sq_acc[...] = part

    @pl.when(step > 0)
    def _():
        acc_ref[...] += term
        if squares:
            sq_acc[...] += part

    @pl.when(step == steps - 1)
    def _():
        out_ref[...] = acc_ref[...].astype(out_ref.dtype)
        if squares:
            sq_ref[...] = jnp.sum(sq_acc[...].T, axis=0, keepdims=True)


def vocab_share(half, embed_table, norm_gain, w_streams, out_dtype, squares):
    vocab, feats = embed_table.shape
    streams, _, local_chans = w_streams.shape
    chans = local_chans // 2
    slabs, steps = 2, 2
    depth = feats // (slabs * steps)
    width = streams * chans
    out_shape = [jax.ShapeDtypeStruct((vocab, width), out_dtype)]
    out_specs = [pl.BlockSpec((vocab, width), lambda k, h: (0, 0))]
    scratch = [pltpu.VMEM((vocab, width), jnp.float32)]
    if squares:
        out_shape.append(jax.ShapeDtypeStruct((1, vocab), jnp.float32))
        out_specs.append(pl.BlockSpec((1, vocab), lambda k, h: (0, 0)))
        scratch.append(pltpu.VMEM((vocab, LANES), jnp.float32))
    emb_spec = lambda j: pl.BlockSpec((vocab, depth), lambda k, h: (0, k * slabs + j))
    w_spec = lambda j: pl.BlockSpec((streams, depth, chans), lambda k, h: (0, k * slabs + j, h[0]))
    return pl.pallas_call(
        functools.partial(vocab_share_body, slabs=slabs, steps=steps, squares=squares),
        grid_spec=pltpu.PrefetchScalarGridSpec(
            num_scalar_prefetch=1,
            grid=(steps,),
            in_specs=[pl.BlockSpec((feats,), lambda k, h: (0,))]
            + [emb_spec(j) for j in range(slabs)]
            + [w_spec(j) for j in range(slabs)],
            out_specs=out_specs,
            scratch_shapes=scratch,
        ),
        out_shape=out_shape,
        compiler_params=pltpu.CompilerParams(vmem_limit_bytes=60 * MIB),
        cost_estimate=pl.CostEstimate(
            flops=2 * vocab * feats * width,
            bytes_accessed=2 * feats * (vocab + width),
            transcendentals=0,
        ),
        name="vocab_share",
    )(half, norm_gain, *([embed_table] * slabs), *([w_streams] * slabs))


def mixer_body(
    place_ref, tok_ref, own_ref, got_ref, sq_ref, sq_got_ref, taps_ref, filt_ref, *refs,
    feature_count, chunk,
):
    hops = len(refs) - 8
    near, far = refs[:hops], refs[hops]
    vocab_t, toeplitz, tap_cols, carry, prod, gate, conv = refs[hops + 1 :]
    chans = far.shape[-1]
    vocab = vocab_t.shape[1]
    blocks = tok_ref.shape[0]
    groups, taps = filt_ref.shape
    gsz = chans // groups
    length = blocks * taps
    genome = pl.program_id(0)

    @pl.when(genome == 0)
    def _():
        sums = (own_ref[...] + got_ref[...].astype(jnp.float32)).T
        scale = lax.rsqrt((sq_ref[...] + sq_got_ref[...]) / feature_count + 1e-06)
        vocab_t[...] = (sums * scale).astype(jnp.bfloat16)
        row = lax.broadcasted_iota(jnp.int32, (taps, taps), 0)
        col = lax.broadcasted_iota(jnp.int32, (taps, taps), 1)
        filt = filt_ref[...].astype(jnp.float32)
        for g in range(groups):
            circ = pltpu.roll(
                jnp.broadcast_to(filt[g : g + 1], (taps, taps)), 0, 1, stride=1, stride_axis=0
            )
            toeplitz[g, :taps] = jnp.where(col < row, circ, 0.0).astype(jnp.bfloat16)
            toeplitz[g, taps:] = jnp.where(col >= row, circ, 0.0).astype(jnp.bfloat16)
        tap_cols[...] = taps_ref[...].T
        prod[:, :gsz, :] = jnp.zeros((groups, gsz, taps), jnp.bfloat16)

    for k in range(2):
        carry[k] = jnp.zeros(carry.shape[1:], jnp.float32)

    ids = lax.broadcasted_iota(jnp.int32, (vocab, chunk), 0)
    lane = lax.broadcasted_iota(jnp.int32, (chans, LANES), 1)
    per = chunk // taps
    for n in range(length // chunk):
        toks = jnp.concatenate(
            [tok_ref[n * per + b, pl.ds(genome, 1), :] for b in range(per)], axis=1
        )
        picks = jnp.where(ids == toks, 1.0, 0.0)
        proj = jnp.dot(vocab_t[...], picks.astype(jnp.bfloat16), preferred_element_type=jnp.float32)
        mixed = []
        for s in range(3):
            cur = proj[s * chans : (s + 1) * chans]
            total = tap_cols[:, s : s + 1] * cur
            for k in (1, 2):
                back = pltpu.roll(cur, k, 1)
                head = jnp.where(lane < k, carry[k - 1, s], back[:, :LANES])
                carry[k - 1, s] = back[:, :LANES]
                back = jnp.concatenate([head, back[:, LANES:]], axis=1)
                total = total + tap_cols[:, 3 * k + s : 3 * k + s + 1] * back
            mixed.append(total)
        inner = (mixed[0] * mixed[2]).astype(jnp.bfloat16)
        for b in range(per):
            gate[n * per + b] = mixed[1][:, b * taps : (b + 1) * taps]
            at = (n * per + b + 1) * gsz
            for g in range(groups):
                prod[g, at : at + gsz, :] = inner[g * gsz : (g + 1) * gsz, b * taps : (b + 1) * taps]
    rows = blocks * gsz
    for g in range(groups):
        pair = jnp.concatenate([prod[g, :rows], prod[g, gsz : gsz + rows]], axis=1)
        conv[g] = jnp.dot(pair, toeplitz[g], preferred_element_type=jnp.float32)
    for r in range(blocks):
        b = place_ref[0] ^ r
        at = pl.ds(pl.multiple_of(b * gsz, gsz), gsz)
        filtered = jnp.concatenate([conv[g, at, :] for g in range(groups)], axis=0)
        gated = (gate[b] * filtered).T.astype(jnp.bfloat16)
        if r & 2:
            far[r >> 2, r & 1, 0] = gated
        else:
            near[r >> 2][r & 1, 0] = gated


def mixer(place, tokens, own, got, squares, squares_got, taps_rows, filt, feature_count):
    blocks, genomes, taps = tokens.shape
    vocab, width = own.shape
    chans = width // 3
    groups, _ = filt.shape
    gsz = chans // groups
    hops = blocks // 4
    length = blocks * taps
    whole = lambda *shape: pl.BlockSpec(shape, lambda g, p: (0,) * len(shape))
    near_shape = (2, genomes, taps, chans)
    return pl.pallas_call(
        functools.partial(mixer_body, feature_count=feature_count, chunk=2 * taps),
        grid_spec=pltpu.PrefetchScalarGridSpec(
            num_scalar_prefetch=1,
            grid=(genomes,),
            in_specs=[
                whole(blocks, genomes, taps),
                whole(vocab, width),
                whole(vocab, width),
                whole(1, vocab),
                whole(1, vocab),
                whole(*taps_rows.shape),
                whole(groups, taps),
            ],
            out_specs=[pl.BlockSpec((2, 1, taps, chans), lambda g, p: (0, g, 0, 0))] * hops
            + [pl.BlockSpec((hops, 2, 1, taps, chans), lambda g, p: (0, 0, g, 0, 0))],
            scratch_shapes=[
                pltpu.VMEM((width, vocab), jnp.bfloat16),
                pltpu.VMEM((groups, 2 * taps, taps), jnp.bfloat16),
                pltpu.VMEM((chans, taps_rows.shape[0]), jnp.float32),
                pltpu.VMEM((2, 3, chans, LANES), jnp.float32),
                pltpu.VMEM((groups, (blocks + 1) * gsz, taps), jnp.bfloat16),
                pltpu.VMEM((blocks, chans, taps), jnp.float32),
                pltpu.VMEM((groups, blocks * gsz, taps), jnp.float32),
            ],
        ),
        out_shape=[jax.ShapeDtypeStruct(near_shape, jnp.bfloat16)] * hops
        + [jax.ShapeDtypeStruct((hops,) + near_shape, jnp.bfloat16)],
        compiler_params=pltpu.CompilerParams(vmem_limit_bytes=26 * MIB),
        cost_estimate=pl.CostEstimate(
            flops=2 * genomes * length * vocab * width,
            bytes_accessed=6 * vocab * width + 2 * genomes * length * chans,
            transcendentals=0,
        ),
        name="mixer",
    )(place, tokens, own, got, squares, squares_got, taps_rows, filt)


def project_body(place_ref, *refs, hops, first):
    mine, other, cross = refs[:hops], refs[hops : 2 * hops], refs[2 * hops]
    weights = refs[2 * hops + 1 : 3 * hops + 1]
    rest = refs[3 * hops + 1 :]
    chans = cross.shape[-1]
    genomes, rows = cross.shape[1:3]
    if first:
        tok_ref, table_ref, out_ref, gated, picks = rest
    else:
        acc_ref, out_ref, gated = rest

    @pl.when(pl.program_id(0) == 0)
    def _():
        core, plane = place_ref[0] & 1, place_ref[1]
        for j in range(hops):
            pieces = (
                (mine[j], 0, core, plane),
                (other[j], 0, core, 1 - plane),
                (cross, j, 1 - core, plane),
                (cross, hops + j, 1 - core, 1 - plane),
            )
            for ref, lead, from_core, from_plane in pieces:
                at = (2 * from_core + from_plane) * chans
                lanes = pl.ds(pl.multiple_of(at, LANES), chans)
                for g in range(genomes):
                    gated[j, g * rows : (g + 1) * rows, lanes] = ref[lead, g]
        if first:
            vocab = table_ref.shape[0]
            toks = tok_ref[place_ref[0]]
            toks = jnp.concatenate([toks[g : g + 1] for g in range(genomes)], axis=1)
            ids = lax.broadcasted_iota(jnp.int32, (vocab, genomes * rows), 0)
            picks[...] = jnp.where(ids == toks, 1.0, 0.0).T.astype(jnp.bfloat16)

    if first:
        total = jnp.dot(picks[...], table_ref[...], preferred_element_type=jnp.float32)
    else:
        total = jnp.concatenate([acc_ref[g] for g in range(genomes)], axis=0)
    for j in range(hops):
        total = total + lax.dot_general(
            gated[j], weights[j][...], (((1,), (1,)), ((), ())), preferred_element_type=jnp.float32
        )
    for g in range(genomes):
        out_ref[g] = total[g * rows : (g + 1) * rows].astype(out_ref.dtype)


def project(place, mine, other, cross, side, w_out, start, out_dtype):
    hops = len(mine)
    columns = [2 * k + side for k in range(hops)]
    other = [other[k] for k in range(hops)]
    first = isinstance(start, tuple)
    _, genomes, rows, chans = cross.shape
    feats = w_out.shape[0]
    tile = 1024
    whole = lambda a: pl.BlockSpec(a.shape, lambda f, p: (0,) * a.ndim)
    slab = pl.BlockSpec((genomes, rows, tile), lambda f, p: (0, 0, f))
    w_spec = lambda c: pl.BlockSpec((tile, 4 * chans), lambda f, p: (f, (p[0] >> 1) ^ c))
    in_specs = [whole(a) for a in mine + other] + [whole(cross)] + [w_spec(c) for c in columns]
    operands = mine + other + [cross] + [w_out] * hops
    scratch = [pltpu.VMEM((hops, genomes * rows, 4 * chans), jnp.bfloat16)]
    depth = hops * 4 * chans
    if first:
        tokens, table = start
        vocab = table.shape[0]
        in_specs += [whole(tokens), pl.BlockSpec((vocab, tile), lambda f, p: (0, f))]
        scratch.append(pltpu.VMEM((genomes * rows, vocab), jnp.bfloat16))
        operands += [tokens, table]
        depth += vocab
    else:
        in_specs.append(slab)
        operands.append(start)
    return pl.pallas_call(
        functools.partial(project_body, hops=hops, first=first),
        grid_spec=pltpu.PrefetchScalarGridSpec(
            num_scalar_prefetch=1,
            grid=(feats // tile,),
            in_specs=in_specs,
            out_specs=slab,
            scratch_shapes=scratch,
        ),
        out_shape=jax.ShapeDtypeStruct((genomes, rows, feats), out_dtype),
        compiler_params=pltpu.CompilerParams(vmem_limit_bytes=26 * MIB),
        cost_estimate=pl.CostEstimate(
            flops=2 * genomes * rows * feats * depth,
            bytes_accessed=2 * feats * depth + 6 * genomes * rows * feats,
            transcendentals=0,
        ),
        name="project",
    )(place, *operands)


def swap_wt(shard):
    return lax.ppermute(shard, "wt", [(0, 1), (1, 0)])


def swap_seq(shard, step):
    return lax.ppermute(shard, "seq", [(i, i ^ step) for i in range(lax.axis_size("seq"))])


def swap_core(mine, other):
    parts = [a[1] for a in mine] + [other[j, 1] for j in range(len(mine))]
    return swap_seq(jnp.stack(parts), 1)


def gather_tokens(tokens):
    size = lax.axis_size("seq") * lax.axis_size("wt")
    copies = jnp.broadcast_to(tokens[None], (size,) + tokens.shape)
    everyone = lax.all_to_all(copies, ("seq", "wt"), 0, 0, tiled=True)
    return everyone.reshape(lax.axis_size("seq"), lax.axis_size("wt"), tokens.shape[1])


def shared_block(tokens, embed_table, norm_gain, w_in, short_taps, filters, w_out):
    me = lax.axis_index("wt")
    local_chans = w_in.shape[2]
    chans = local_chans // 2
    groups = filters.shape[0] // 2
    feature_count = embed_table.shape[1] * lax.axis_size("wt")
    w_streams = jnp.transpose(w_in, (1, 0, 2))
    place = jnp.stack([lax.axis_index("seq"), me]).astype(jnp.int32)
    pick = lambda which: jnp.reshape(which, (1,)).astype(jnp.int32)
    sent, squares = vocab_share(
        pick(1 - me), embed_table, norm_gain, w_streams, jnp.bfloat16, True
    )
    tokens, sent, squares = lax.optimization_barrier((tokens, sent, squares))
    got = swap_wt(sent)
    squares_got = swap_wt(squares)
    all_tokens = gather_tokens(tokens)
    (own,) = vocab_share(pick(me), embed_table, norm_gain, w_streams, jnp.float32, False)
    taps_rows = lax.dynamic_slice_in_dim(
        short_taps.astype(jnp.float32).reshape(9, local_chans), me * chans, chans, 1
    )
    taps_rows = jnp.pad(taps_rows, ((0, 7), (0, 0)))
    filt = lax.dynamic_slice_in_dim(filters, me * groups, groups, 0)
    *near, far = mixer(
        place, all_tokens, own, got, squares, squares_got, taps_rows, filt, feature_count
    )
    hops = len(near)
    order = sorted(range(1, hops), key=lambda k: (k == 1, k))
    arrived = swap_seq(far, 2)
    near_side = near[:1] + [None] * (hops - 1)
    far_side = [arrived[0]] + [None] * (hops - 1)
    for k in order:
        near_side[k] = swap_seq(near[k], 4 * k)
    for k in order:
        far_side[k] = swap_seq(arrived[k], 4 * k)
    near_other = swap_wt(jnp.stack(near_side))
    near_cross = swap_core(near_side, near_other)
    far_other = swap_wt(jnp.stack(far_side))
    near_cross, _ = lax.optimization_barrier((near_cross, far_side[1]))
    total = project(
        place, near_side, near_other, near_cross, 0, w_out, (all_tokens, embed_table), jnp.float32
    )
    far_other, total = lax.optimization_barrier((far_other, total))
    far_cross = swap_core(far_side, far_other)
    return project(place, far_side, far_other, far_cross, 1, w_out, total, jnp.bfloat16)


def local(*args):
    tokens, embed_table, norm_gain, w_in, short_taps, filters, w_out = args
    ranks = lax.axis_size("seq")
    wide = lax.axis_size("wt") == 2 and w_in.shape[2] == 2 * LANES and ranks in (8, 16, 32)
    aligned = tokens.shape[1] == filters.shape[1] == LANES and w_out.shape[0] % 1024 == 0
    if wide and aligned and tokens.shape[0] == 1:
        return shared_block(*args)
    return plain_block(*args)


def solution(mesh):
    placed = (
        P("wt", "seq"),
        P(None, "wt"),
        P("wt"),
        P("wt", None, "seq"),
        P(None, None, "seq"),
        P("seq", None),
        P("wt", None),
    )
    return jax.shard_map(
        local, mesh=mesh, in_specs=placed, out_specs=P(None, "seq", "wt"), check_vma=False
    )
```

```python
import functools

import jax
import jax.numpy as jnp
from jax import lax
from jax.experimental import pallas as pl
from jax.experimental.pallas import tpu as pltpu
from jax.sharding import PartitionSpec as P

LANES = 128
SQ_ROWS = 16
MIB = 1 << 20


def shifted(shard, axis, by):
    size = lax.axis_size(axis)
    pairs = [(i, i + by) for i in range(size) if 0 <= i + by < size]
    return lax.ppermute(shard, axis, pairs)


def causal_pair(filter_vals):
    tap_count = filter_vals.shape[1]
    group_count = filter_vals.shape[0]
    tiled_taps = jnp.tile(filter_vals, (1, 2 * tap_count - 1)).reshape(
        group_count, tap_count, 2 * tap_count - 1
    )[:, :, :tap_count]
    circulant = jnp.swapaxes(tiled_taps, 1, 2)
    row_pos = lax.broadcasted_iota(jnp.int32, (tap_count, tap_count), 0)
    col_pos = lax.broadcasted_iota(jnp.int32, (tap_count, tap_count), 1)
    lower_mask = (row_pos >= col_pos)[None]
    zero_mat = jnp.zeros_like(circulant)
    return (jnp.where(lower_mask, circulant, zero_mat), jnp.where(lower_mask, zero_mat, circulant))


def short_mix(extended, tap_vals):
    row_count = extended.shape[0] - 2
    ext_vals = extended.astype(jnp.float32)
    return (
        tap_vals[0] * ext_vals[2 : 2 + row_count]
        + tap_vals[1] * ext_vals[1 : 1 + row_count]
        + tap_vals[2] * ext_vals[0:row_count]
    )


def run_filter(extended, lower_mat, upper_mat):
    tap_count = lower_mat.shape[1]
    group_count = lower_mat.shape[0]
    chan_count = extended.shape[1]
    blocks = extended.shape[0] // tap_count
    stacked = extended.reshape(blocks, tap_count, group_count, chan_count // group_count)
    filtered = jnp.einsum(
        "gij,bjgc->bigc", lower_mat, stacked[1:], preferred_element_type=jnp.float32
    )
    filtered = filtered + jnp.einsum(
        "gij,bjgc->bigc", upper_mat, stacked[:-1], preferred_element_type=jnp.float32
    )
    return filtered.reshape((blocks - 1) * tap_count, chan_count)


def plain_block(tokens, embed_table, norm_gain, w_in, short_taps, filters, w_out):
    token_ids = tokens[0]
    own_len = token_ids.shape[0]
    tap_count = filters.shape[1]
    table_vals = embed_table.astype(jnp.float32)
    square_sums = lax.psum(jnp.sum(table_vals * table_vals, axis=1, keepdims=True), "wt")
    feature_count = embed_table.shape[1] * lax.axis_size("wt")
    row_scale = lax.rsqrt(square_sums / feature_count + 1e-06)
    normed = (table_vals * row_scale * norm_gain.astype(jnp.float32)).astype(jnp.bfloat16)
    local_chans = w_in.shape[2]
    w_flat = w_in.reshape(w_in.shape[0], 3 * local_chans)
    vocab_size = embed_table.shape[0]
    partial_sum = jnp.dot(normed, w_flat, preferred_element_type=jnp.float32)
    vocab_flat = lax.psum(partial_sum, "wt").astype(jnp.bfloat16)
    vocab_proj = vocab_flat.reshape(vocab_size, 3, local_chans)
    vocab_all, tap_all, filter_all = (
        lax.all_gather(vocab_proj, "seq", axis=2, tiled=True),
        lax.all_gather(short_taps, "seq", axis=2, tiled=True),
        lax.all_gather(filters, "seq", axis=0, tiled=True),
    )
    projected = jnp.take(vocab_all, token_ids, axis=0)
    edge_prev = shifted(projected[own_len - 2 :], "seq", 1)
    mixture = short_mix(
        jnp.concatenate([edge_prev, projected], axis=0), tap_all.astype(jnp.float32)
    )
    product = (mixture[:, 0] * mixture[:, 2]).astype(jnp.bfloat16)
    tail_prev = shifted(product[own_len - tap_count + 1 :], "seq", 1)
    chan_count = product.shape[1]
    extended = jnp.concatenate(
        [jnp.zeros((1, chan_count), jnp.bfloat16), tail_prev, product], axis=0
    )
    lower_mat, upper_mat = causal_pair(filter_all)
    filtered = run_filter(extended, lower_mat, upper_mat)
    gated = (mixture[:, 1] * filtered).astype(jnp.bfloat16)
    everyone = lax.all_gather(tokens, "wt", axis=0, tiled=True)
    branch = jnp.einsum(
        "knc,dc->knd",
        lax.all_gather(gated[None], "wt", axis=0, tiled=True),
        w_out,
        preferred_element_type=jnp.float32,
    )
    embedded = jnp.take(embed_table, everyone, axis=0)
    return (embedded.astype(jnp.float32) + branch).astype(jnp.bfloat16)


def three_parts(vals):
    parts = []
    for _ in range(3):
        parts.append(vals.astype(jnp.bfloat16).astype(jnp.float32))
        vals = vals - parts[-1]
    return parts


def vocab_share_body(half_ref, gain_ref, *refs, slabs, steps, squares):
    embs, weights = refs[:slabs], refs[slabs : 2 * slabs]
    if squares:
        tok_ref, out_ref, sq_ref, copies_ref, acc_ref, sq_acc = refs[2 * slabs :]
    else:
        out_ref, acc_ref = refs[2 * slabs :]
    step = pl.program_id(0)
    depth = embs[0].shape[1]
    term = part = None
    for j in range(slabs):
        emb = embs[j][...]
        at = pl.multiple_of((step * slabs + j) * depth, LANES)
        scaled = emb * gain_ref[pl.ds(at, depth)][None]
        wide = jnp.concatenate([weights[j][s] for s in range(weights[j].shape[0])], axis=1)
        more = jnp.dot(scaled, wide, preferred_element_type=jnp.float32)
        term = more if term is None else term + more
        if squares:
            vals = emb.astype(jnp.float32)
            vals = vals * vals
            for i in range(depth // LANES):
                piece = vals[:, i * LANES : (i + 1) * LANES]
                part = piece if part is None else part + piece

    @pl.when(step == 0)
    def _():
        acc_ref[...] = term
        if squares:
            sq_acc[...] = part

    @pl.when(step > 0)
    def _():
        acc_ref[...] += term
        if squares:
            sq_acc[...] += part

    @pl.when(step == steps - 1)
    def _():
        vocab = acc_ref.shape[0]
        out_ref[:vocab] = acc_ref[...].astype(out_ref.dtype)
        if squares:
            sums = jnp.sum(sq_acc[...].T, axis=0, keepdims=True)
            sq_ref[...] = sums
            tail = jnp.zeros((SQ_ROWS, vocab), jnp.float32)
            row = lax.broadcasted_iota(jnp.int32, tail.shape, 0)
            for i, piece in enumerate(three_parts(sums)):
                tail = jnp.where(row == i, piece, tail)
            for i in range(vocab // LANES):
                at = vocab + (i // 2) * SQ_ROWS
                out_ref[at : at + SQ_ROWS, (i % 2) * LANES : (i % 2 + 1) * LANES] = tail[
                    :, i * LANES : (i + 1) * LANES
                ].astype(out_ref.dtype)
            copies_ref[...] = jnp.broadcast_to(tok_ref[...][None], copies_ref.shape)


def vocab_share(half, embed_table, norm_gain, w_streams, out_dtype, tokens=None, ranks=0):
    squares = tokens is not None
    vocab, feats = embed_table.shape
    streams, _, local_chans = w_streams.shape
    chans = local_chans // 2
    slabs, steps = 2, 2
    depth = feats // (slabs * steps)
    width = streams * chans
    whole = lambda *shape: pl.BlockSpec(shape, lambda k, h: (0,) * len(shape))
    rows = vocab + (SQ_ROWS * vocab // (2 * LANES) if squares else 0)
    out_shape = [jax.ShapeDtypeStruct((rows, width), out_dtype)]
    scratch = [pltpu.VMEM((vocab, width), jnp.float32)]
    extra_specs, extra = [], []
    if squares:
        extra_specs, extra = [whole(*tokens.shape)], [tokens]
        out_shape.append(jax.ShapeDtypeStruct((1, vocab), jnp.float32))
        out_shape.append(jax.ShapeDtypeStruct((ranks,) + tokens.shape, tokens.dtype))
        scratch.append(pltpu.VMEM((vocab, LANES), jnp.float32))
    emb_spec = lambda j: pl.BlockSpec((vocab, depth), lambda k, h: (0, k * slabs + j))
    w_spec = lambda j: pl.BlockSpec((streams, depth, chans), lambda k, h: (0, k * slabs + j, h[0]))
    return pl.pallas_call(
        functools.partial(vocab_share_body, slabs=slabs, steps=steps, squares=squares),
        grid_spec=pltpu.PrefetchScalarGridSpec(
            num_scalar_prefetch=1,
            grid=(steps,),
            in_specs=[pl.BlockSpec((feats,), lambda k, h: (0,))]
            + [emb_spec(j) for j in range(slabs)]
            + [w_spec(j) for j in range(slabs)]
            + extra_specs,
            out_specs=[whole(*a.shape) for a in out_shape],
            scratch_shapes=scratch,
        ),
        out_shape=out_shape,
        compiler_params=pltpu.CompilerParams(vmem_limit_bytes=60 * MIB),
        name="vocab_share",
    )(half, norm_gain, *([embed_table] * slabs), *([w_streams] * slabs), *extra)


def mixer_body(
    place_ref, tok_ref, own_ref, got_ref, sq_ref, taps_ref, filt_ref, *refs,
    feature_count, chunk,
):
    home, *near, far = refs[:-7]
    vocab_t, toeplitz, tap_cols, carry, prod, gate, conv = refs[-7:]
    chans = far.shape[-1]
    vocab = vocab_t.shape[1]
    blocks = tok_ref.shape[0]
    groups, taps = filt_ref.shape
    gsz = chans // groups
    length = blocks * taps
    genome = pl.program_id(0)

    @pl.when(genome == 0)
    def _():
        sums = (own_ref[...] + got_ref[:vocab].astype(jnp.float32)).T
        tails = []
        for i in range(vocab // LANES):
            at = vocab + (i // 2) * SQ_ROWS
            tail = got_ref[at : at + SQ_ROWS, (i % 2) * LANES : (i % 2 + 1) * LANES]
            tail = tail.astype(jnp.float32)
            tails.append(tail[0:1] + tail[1:2] + tail[2:3])
        squares = sq_ref[...] + jnp.concatenate(tails, axis=1)
        scale = lax.rsqrt(squares / feature_count + 1e-06)
        vocab_t[...] = (sums * scale).astype(jnp.bfloat16)
        row = lax.broadcasted_iota(jnp.int32, (taps, taps), 0)
        col = lax.broadcasted_iota(jnp.int32, (taps, taps), 1)
        filt = filt_ref[...].astype(jnp.float32)
        for g in range(groups):
            circ = pltpu.roll(
                jnp.broadcast_to(filt[g : g + 1], (taps, taps)), 0, 1, stride=1, stride_axis=0
            )
            toeplitz[g, :taps] = jnp.where(col < row, circ, 0.0).astype(jnp.bfloat16)
            toeplitz[g, taps:] = jnp.where(col >= row, circ, 0.0).astype(jnp.bfloat16)
        tap_cols[...] = taps_ref[...].T
        prod[:, :gsz, :] = jnp.zeros((groups, gsz, taps), jnp.bfloat16)

    for k in range(2):
        carry[k] = jnp.zeros(carry.shape[1:], jnp.float32)

    ids = lax.broadcasted_iota(jnp.int32, (vocab, chunk), 0)
    lane = lax.broadcasted_iota(jnp.int32, (chans, LANES), 1)
    per = chunk // taps
    for n in range(length // chunk):
        toks = jnp.concatenate(
            [tok_ref[n * per + b, pl.ds(genome, 1), :] for b in range(per)], axis=1
        )
        picks = jnp.where(ids == toks, 1.0, 0.0)
        proj = jnp.dot(vocab_t[...], picks.astype(jnp.bfloat16), preferred_element_type=jnp.float32)
        mixed = []
        for s in range(3):
            cur = proj[s * chans : (s + 1) * chans]
            total = tap_cols[:, s : s + 1] * cur
            for k in (1, 2):
                back = pltpu.roll(cur, k, 1)
                head = jnp.where(lane < k, carry[k - 1, s], back[:, :LANES])
                carry[k - 1, s] = back[:, :LANES]
                back = jnp.concatenate([head, back[:, LANES:]], axis=1)
                total = total + tap_cols[:, 3 * k + s : 3 * k + s + 1] * back
            mixed.append(total)
        inner = (mixed[0] * mixed[2]).astype(jnp.bfloat16)
        for b in range(per):
            gate[n * per + b] = mixed[1][:, b * taps : (b + 1) * taps]
            at = (n * per + b + 1) * gsz
            for g in range(groups):
                prod[g, at : at + gsz, :] = inner[g * gsz : (g + 1) * gsz, b * taps : (b + 1) * taps]
    rows = blocks * gsz
    for g in range(groups):
        pair = jnp.concatenate([prod[g, :rows], prod[g, gsz : gsz + rows]], axis=1)
        conv[g] = jnp.dot(pair, toeplitz[g], preferred_element_type=jnp.float32)
    for r in range(blocks):
        b = place_ref[0] ^ r
        at = pl.ds(pl.multiple_of(b * gsz, gsz), gsz)
        filtered = jnp.concatenate([conv[g, at, :] for g in range(groups)], axis=0)
        gated = (gate[b] * filtered).T.astype(jnp.bfloat16)
        k, dx, dc = r >> 2, (r >> 1) & 1, r & 1
        if k == 0:
            home[dx, dc, 0] = gated
        elif dx == 1:
            far[k - 1, dc, 0] = gated
        else:
            near[k - 1][dc, 0] = gated


def mixer(place, tokens, own, got, squares, taps_rows, filt, feature_count):
    blocks, genomes, taps = tokens.shape
    vocab, width = own.shape
    chans = width // 3
    groups, _ = filt.shape
    gsz = chans // groups
    hops = blocks // 4
    length = blocks * taps
    whole = lambda *shape: pl.BlockSpec(shape, lambda g, p: (0,) * len(shape))
    near_shape = (2, genomes, taps, chans)
    packs = lambda n: pl.BlockSpec((n, 2, 1, taps, chans), lambda g, p: (0, 0, g, 0, 0))
    return pl.pallas_call(
        functools.partial(mixer_body, feature_count=feature_count, chunk=2 * taps),
        grid_spec=pltpu.PrefetchScalarGridSpec(
            num_scalar_prefetch=1,
            grid=(genomes,),
            in_specs=[
                whole(blocks, genomes, taps),
                whole(vocab, width),
                whole(*got.shape),
                whole(1, vocab),
                whole(*taps_rows.shape),
                whole(groups, taps),
            ],
            out_specs=[packs(2)]
            + [pl.BlockSpec((2, 1, taps, chans), lambda g, p: (0, g, 0, 0))] * (hops - 1)
            + [packs(hops - 1)],
            scratch_shapes=[
                pltpu.VMEM((width, vocab), jnp.bfloat16),
                pltpu.VMEM((groups, 2 * taps, taps), jnp.bfloat16),
                pltpu.VMEM((chans, taps_rows.shape[0]), jnp.float32),
                pltpu.VMEM((2, 3, chans, LANES), jnp.float32),
                pltpu.VMEM((groups, (blocks + 1) * gsz, taps), jnp.bfloat16),
                pltpu.VMEM((blocks, chans, taps), jnp.float32),
                pltpu.VMEM((groups, blocks * gsz, taps), jnp.float32),
            ],
        ),
        out_shape=[jax.ShapeDtypeStruct((2,) + near_shape, jnp.bfloat16)]
        + [jax.ShapeDtypeStruct(near_shape, jnp.bfloat16)] * (hops - 1)
        + [jax.ShapeDtypeStruct((hops - 1,) + near_shape, jnp.bfloat16)],
        compiler_params=pltpu.CompilerParams(vmem_limit_bytes=26 * MIB),
        cost_estimate=pl.CostEstimate(
            flops=2 * genomes * length * vocab * width,
            bytes_accessed=6 * vocab * width + 2 * genomes * length * chans,
            transcendentals=0,
        ),
        name="mixer",
    )(place, tokens, own, got, squares, taps_rows, filt)


def project_body(place_ref, *refs, columns, first, last, tile):
    hops = len(columns)
    mine, other, cross, w_hbm = refs[:hops], refs[hops : 2 * hops], refs[2 * hops], refs[2 * hops + 1]
    rest = refs[2 * hops + 2 :]
    if first:
        tok_ref, table_ref, out_ref, gated, slabs, arrivals, picks = rest
    elif last:
        acc_ref, out_ref, gated, slabs, arrivals, ready, leaving = rest
    else:
        acc_ref, out_ref, gated, slabs, arrivals = rest
    chans = cross.shape[-1]
    genomes, rows = cross.shape[1:3]
    wide = 4 * chans
    tiles = w_hbm.shape[0] // tile
    arriving = []
    for t in range(tiles):
        for j, c in enumerate(columns):
            at = pl.multiple_of(((place_ref[0] >> 1) ^ c) * wide, wide)
            copy = pltpu.make_async_copy(
                w_hbm.at[pl.ds(t * tile, tile), pl.ds(at, wide)],
                slabs.at[t, :, pl.ds(j * wide, wide)],
                arrivals.at[t, j],
            )
            copy.start()
            arriving.append(copy)

    core, plane = place_ref[0] & 1, place_ref[1]
    for j in range(hops):
        pieces = (
            (mine[j], 0, core, plane),
            (other[j], 0, core, 1 - plane),
            (cross, j, 1 - core, plane),
            (cross, hops + j, 1 - core, 1 - plane),
        )
        for ref, lead, from_core, from_plane in pieces:
            at = j * wide + (2 * from_core + from_plane) * chans
            lanes = pl.ds(pl.multiple_of(at, LANES), chans)
            for g in range(genomes):
                gated[g * rows : (g + 1) * rows, lanes] = ref[lead, g]
    if first:
        vocab = table_ref.shape[0]
        toks = tok_ref[place_ref[0]]
        toks = jnp.concatenate([toks[g : g + 1] for g in range(genomes)], axis=1)
        ids = lax.broadcasted_iota(jnp.int32, (vocab, genomes * rows), 0)
        picks[...] = jnp.where(ids == toks, 1.0, 0.0).T.astype(jnp.bfloat16)

    sending = []
    for t in range(tiles):
        at = slice(t * tile, (t + 1) * tile)
        for j in range(hops):
            arriving[t * hops + j].wait()
        total = lax.dot_general(
            gated[...], slabs[t], (((1,), (1,)), ((), ())), preferred_element_type=jnp.float32
        )
        if first:
            total = total + jnp.dot(
                picks[...], table_ref[:, at], preferred_element_type=jnp.float32
            )
        for g in range(genomes):
            part = total[g * rows : (g + 1) * rows]
            if not first:
                part = part + acc_ref[g, :, at]
            if last:
                ready[g, :, at] = part.astype(ready.dtype)
            else:
                out_ref[g, :, at] = part
        if last:
            copy = pltpu.make_async_copy(ready.at[:, :, at], out_ref.at[:, :, at], leaving.at[t])
            copy.start()
            sending.append(copy)
    for copy in sending:
        copy.wait()


def project(place, mine, other, cross, columns, w_out, start, last=False):
    hops = len(mine)
    first = isinstance(start, tuple)
    _, genomes, rows, chans = cross.shape
    feats = w_out.shape[0]
    tile = 1024
    tiles = feats // tile
    vmem = pl.BlockSpec(memory_space=pltpu.VMEM)
    anywhere = pl.BlockSpec(memory_space=pl.ANY)
    operands = mine + other + [cross, w_out]
    in_specs = [pl.BlockSpec(memory_space=pltpu.SMEM)] + [vmem] * (2 * hops + 1) + [anywhere]
    scratch = [
        pltpu.VMEM((genomes * rows, hops * 4 * chans), jnp.bfloat16),
        pltpu.VMEM((tiles, tile, hops * 4 * chans), jnp.bfloat16),
        pltpu.SemaphoreType.DMA((tiles, hops)),
    ]
    if first:
        operands += list(start)
        in_specs += [vmem, vmem]
        scratch.append(pltpu.VMEM((genomes * rows, start[1].shape[0]), jnp.bfloat16))
    else:
        operands.append(start)
        in_specs.append(vmem)
    shape = (genomes, rows, feats)
    if last:
        scratch += [pltpu.VMEM(shape, jnp.bfloat16), pltpu.SemaphoreType.DMA((tiles,))]
    return pl.pallas_call(
        functools.partial(project_body, columns=columns, first=first, last=last, tile=tile),
        in_specs=in_specs,
        out_specs=anywhere if last else vmem,
        scratch_shapes=scratch,
        out_shape=jax.ShapeDtypeStruct(shape, jnp.bfloat16 if last else jnp.float32),
        compiler_params=pltpu.CompilerParams(vmem_limit_bytes=40 * MIB),
        cost_estimate=pl.CostEstimate(
            flops=2 * genomes * rows * feats * hops * 4 * chans,
            bytes_accessed=2 * feats * hops * 4 * chans + 6 * genomes * rows * feats,
            transcendentals=0,
        ),
        name="project",
    )(place, *operands)


def swap_wt(shard):
    return lax.ppermute(shard, "wt", [(0, 1), (1, 0)])


def swap_seq(shard, step):
    return lax.ppermute(shard, "seq", [(i, i ^ step) for i in range(lax.axis_size("seq"))])


def swap_core(mine, other):
    return swap_seq(jnp.stack([a[1] for a in mine + other]), 1)


def shared_block(tokens, embed_table, norm_gain, w_in, short_taps, filters, w_out):
    me = lax.axis_index("wt")
    local_chans = w_in.shape[2]
    chans = local_chans // 2
    groups = filters.shape[0] // 2
    feature_count = embed_table.shape[1] * lax.axis_size("wt")
    w_streams = jnp.transpose(w_in, (1, 0, 2))
    place = jnp.stack([lax.axis_index("seq"), me]).astype(jnp.int32)
    pick = lambda which: jnp.reshape(which, (1,)).astype(jnp.int32)
    seqs, planes = lax.axis_size("seq"), lax.axis_size("wt")
    sent, squares, copies = vocab_share(
        pick(1 - me), embed_table, norm_gain, w_streams, jnp.bfloat16, tokens, seqs * planes
    )
    got = swap_wt(sent)
    all_tokens = lax.all_to_all(copies, ("seq", "wt"), 0, 0, tiled=True)
    all_tokens = all_tokens.reshape(seqs, planes, tokens.shape[1])
    (own,) = vocab_share(pick(me), embed_table, norm_gain, w_streams, jnp.float32)
    taps_rows = lax.dynamic_slice_in_dim(
        short_taps.astype(jnp.float32).reshape(9, local_chans), me * chans, chans, 1
    )
    taps_rows = jnp.pad(taps_rows, ((0, 7), (0, 0)))
    filt = lax.dynamic_slice_in_dim(filters, me * groups, groups, 0)
    home, *near, far = mixer(
        place, all_tokens, own, got, squares, taps_rows, filt, feature_count
    )
    hops = len(near) + 1
    order = sorted(range(1, hops), key=lambda k: (k == 1, k))
    bar = lax.optimization_barrier
    arrived = swap_seq(far, 2)
    home_other = swap_wt(home)
    near_mine = {k: swap_seq(near[k - 1], 4 * k) for k in order}
    far_mine = {k: swap_seq(arrived[k - 1], 4 * k) for k in order}
    crossed = swap_seq(jnp.stack([home[1], home_other[1]]), 2)
    first_mine, first_other = [home[0]], [home_other[0]]
    cross = swap_core(first_mine, first_other)
    total = project(
        place, first_mine, first_other, cross, [0], w_out, (all_tokens, embed_table)
    )
    near_mine = [near_mine[k] for k in range(1, hops)]
    near_other = swap_wt(jnp.stack(near_mine))
    near_mine = [crossed[0]] + near_mine
    near_other = [crossed[1]] + [near_other[k] for k in range(hops - 1)]
    cross = swap_core(near_mine, near_other)
    far_mine = [far_mine[k] for k in range(1, hops)]
    far_mine, cross = bar((far_mine, cross))
    far_other = swap_wt(jnp.stack(far_mine))
    columns = [1] + [2 * k for k in range(1, hops)]
    total, _ = bar((total, far_mine))
    total = project(place, near_mine, near_other, cross, columns, w_out, total)
    far_other, total = bar((far_other, total))
    far_other = [far_other[k] for k in range(hops - 1)]
    cross = swap_core(far_mine, far_other)
    columns = [2 * k + 1 for k in range(1, hops)]
    return project(place, far_mine, far_other, cross, columns, w_out, total, True)


def local(*args):
    tokens, embed_table, norm_gain, w_in, short_taps, filters, w_out = args
    ranks = lax.axis_size("seq")
    wide = lax.axis_size("wt") == 2 and w_in.shape[2] == 2 * LANES and ranks in (8, 16, 32)
    aligned = tokens.shape[1] == filters.shape[1] == LANES and w_out.shape[0] % 1024 == 0
    if wide and aligned and tokens.shape[0] == 1:
        return shared_block(*args)
    return plain_block(*args)


def solution(mesh):
    placed = (
        P("wt", "seq"),
        P(None, "wt"),
        P("wt"),
        P("wt", None, "seq"),
        P(None, None, "seq"),
        P("seq", None),
        P("wt", None),
    )
    return jax.shard_map(
        local, mesh=mesh, in_specs=placed, out_specs=P(None, "seq", "wt"), check_vma=False
    )
```

```python
import functools

import jax
import jax.numpy as jnp
from jax import lax
from jax.experimental import pallas as pl
from jax.experimental.pallas import tpu as pltpu
from jax.sharding import PartitionSpec as P

LANES = 128
SQ_ROWS = 16
MIB = 1 << 20


def shifted(shard, axis, by):
    size = lax.axis_size(axis)
    pairs = [(i, i + by) for i in range(size) if 0 <= i + by < size]
    return lax.ppermute(shard, axis, pairs)


def causal_pair(filter_vals):
    tap_count = filter_vals.shape[1]
    group_count = filter_vals.shape[0]
    tiled_taps = jnp.tile(filter_vals, (1, 2 * tap_count - 1)).reshape(
        group_count, tap_count, 2 * tap_count - 1
    )[:, :, :tap_count]
    circulant = jnp.swapaxes(tiled_taps, 1, 2)
    row_pos = lax.broadcasted_iota(jnp.int32, (tap_count, tap_count), 0)
    col_pos = lax.broadcasted_iota(jnp.int32, (tap_count, tap_count), 1)
    lower_mask = (row_pos >= col_pos)[None]
    zero_mat = jnp.zeros_like(circulant)
    return (jnp.where(lower_mask, circulant, zero_mat), jnp.where(lower_mask, zero_mat, circulant))


def short_mix(extended, tap_vals):
    row_count = extended.shape[0] - 2
    ext_vals = extended.astype(jnp.float32)
    return (
        tap_vals[0] * ext_vals[2 : 2 + row_count]
        + tap_vals[1] * ext_vals[1 : 1 + row_count]
        + tap_vals[2] * ext_vals[0:row_count]
    )


def run_filter(extended, lower_mat, upper_mat):
    tap_count = lower_mat.shape[1]
    group_count = lower_mat.shape[0]
    chan_count = extended.shape[1]
    blocks = extended.shape[0] // tap_count
    stacked = extended.reshape(blocks, tap_count, group_count, chan_count // group_count)
    filtered = jnp.einsum(
        "gij,bjgc->bigc", lower_mat, stacked[1:], preferred_element_type=jnp.float32
    )
    filtered = filtered + jnp.einsum(
        "gij,bjgc->bigc", upper_mat, stacked[:-1], preferred_element_type=jnp.float32
    )
    return filtered.reshape((blocks - 1) * tap_count, chan_count)


def plain_block(tokens, embed_table, norm_gain, w_in, short_taps, filters, w_out):
    token_ids = tokens[0]
    own_len = token_ids.shape[0]
    tap_count = filters.shape[1]
    table_vals = embed_table.astype(jnp.float32)
    square_sums = lax.psum(jnp.sum(table_vals * table_vals, axis=1, keepdims=True), "wt")
    feature_count = embed_table.shape[1] * lax.axis_size("wt")
    row_scale = lax.rsqrt(square_sums / feature_count + 1e-06)
    normed = (table_vals * row_scale * norm_gain.astype(jnp.float32)).astype(jnp.bfloat16)
    local_chans = w_in.shape[2]
    w_flat = w_in.reshape(w_in.shape[0], 3 * local_chans)
    vocab_size = embed_table.shape[0]
    partial_sum = jnp.dot(normed, w_flat, preferred_element_type=jnp.float32)
    vocab_flat = lax.psum(partial_sum, "wt").astype(jnp.bfloat16)
    vocab_proj = vocab_flat.reshape(vocab_size, 3, local_chans)
    vocab_all, tap_all, filter_all = (
        lax.all_gather(vocab_proj, "seq", axis=2, tiled=True),
        lax.all_gather(short_taps, "seq", axis=2, tiled=True),
        lax.all_gather(filters, "seq", axis=0, tiled=True),
    )
    projected = jnp.take(vocab_all, token_ids, axis=0)
    edge_prev = shifted(projected[own_len - 2 :], "seq", 1)
    mixture = short_mix(
        jnp.concatenate([edge_prev, projected], axis=0), tap_all.astype(jnp.float32)
    )
    product = (mixture[:, 0] * mixture[:, 2]).astype(jnp.bfloat16)
    tail_prev = shifted(product[own_len - tap_count + 1 :], "seq", 1)
    chan_count = product.shape[1]
    extended = jnp.concatenate(
        [jnp.zeros((1, chan_count), jnp.bfloat16), tail_prev, product], axis=0
    )
    lower_mat, upper_mat = causal_pair(filter_all)
    filtered = run_filter(extended, lower_mat, upper_mat)
    gated = (mixture[:, 1] * filtered).astype(jnp.bfloat16)
    everyone = lax.all_gather(tokens, "wt", axis=0, tiled=True)
    branch = jnp.einsum(
        "knc,dc->knd",
        lax.all_gather(gated[None], "wt", axis=0, tiled=True),
        w_out,
        preferred_element_type=jnp.float32,
    )
    embedded = jnp.take(embed_table, everyone, axis=0)
    return (embedded.astype(jnp.float32) + branch).astype(jnp.bfloat16)


def three_parts(vals):
    parts = []
    for _ in range(3):
        parts.append(vals.astype(jnp.bfloat16).astype(jnp.float32))
        vals = vals - parts[-1]
    return parts


def vocab_share_body(half_ref, gain_ref, *refs, slabs, steps, squares):
    embs, weights = refs[:slabs], refs[slabs : 2 * slabs]
    if squares:
        tok_ref, out_ref, sq_ref, copies_ref, acc_ref, sq_acc = refs[2 * slabs :]
    else:
        out_ref, acc_ref = refs[2 * slabs :]
    step = pl.program_id(0)
    depth = embs[0].shape[1]
    term = part = None
    for j in range(slabs):
        emb = embs[j][...]
        at = pl.multiple_of((step * slabs + j) * depth, LANES)
        scaled = emb * gain_ref[pl.ds(at, depth)][None]
        wide = jnp.concatenate([weights[j][s] for s in range(weights[j].shape[0])], axis=1)
        more = jnp.dot(scaled, wide, preferred_element_type=jnp.float32)
        term = more if term is None else term + more
        if squares:
            vals = emb.astype(jnp.float32)
            vals = vals * vals
            for i in range(depth // LANES):
                piece = vals[:, i * LANES : (i + 1) * LANES]
                part = piece if part is None else part + piece

    @pl.when(step == 0)
    def _():
        acc_ref[...] = term
        if squares:
            sq_acc[...] = part

    @pl.when(step > 0)
    def _():
        acc_ref[...] += term
        if squares:
            sq_acc[...] += part

    @pl.when(step == steps - 1)
    def _():
        vocab = acc_ref.shape[0]
        out_ref[:vocab] = acc_ref[...].astype(out_ref.dtype)
        if squares:
            sums = jnp.sum(sq_acc[...].T, axis=0, keepdims=True)
            sq_ref[...] = sums
            tail = jnp.zeros((SQ_ROWS, vocab), jnp.float32)
            row = lax.broadcasted_iota(jnp.int32, tail.shape, 0)
            for i, piece in enumerate(three_parts(sums)):
                tail = jnp.where(row == i, piece, tail)
            for i in range(vocab // LANES):
                at = vocab + (i // 2) * SQ_ROWS
                out_ref[at : at + SQ_ROWS, (i % 2) * LANES : (i % 2 + 1) * LANES] = tail[
                    :, i * LANES : (i + 1) * LANES
                ].astype(out_ref.dtype)
            copies_ref[...] = jnp.broadcast_to(tok_ref[...][None], copies_ref.shape)


def vocab_share(half, embed_table, norm_gain, w_streams, out_dtype, tokens=None, ranks=0):
    squares = tokens is not None
    vocab, feats = embed_table.shape
    streams, _, local_chans = w_streams.shape
    chans = local_chans // 2
    slabs, steps = 2, 2
    depth = feats // (slabs * steps)
    width = streams * chans
    whole = lambda *shape: pl.BlockSpec(shape, lambda k, h: (0,) * len(shape))
    rows = vocab + (SQ_ROWS * vocab // (2 * LANES) if squares else 0)
    out_shape = [jax.ShapeDtypeStruct((rows, width), out_dtype)]
    scratch = [pltpu.VMEM((vocab, width), jnp.float32)]
    extra_specs, extra = [], []
    if squares:
        extra_specs, extra = [whole(*tokens.shape)], [tokens]
        out_shape.append(jax.ShapeDtypeStruct((1, vocab), jnp.float32))
        out_shape.append(jax.ShapeDtypeStruct((ranks,) + tokens.shape, tokens.dtype))
        scratch.append(pltpu.VMEM((vocab, LANES), jnp.float32))
    emb_spec = lambda j: pl.BlockSpec((vocab, depth), lambda k, h: (0, k * slabs + j))
    w_spec = lambda j: pl.BlockSpec((streams, depth, chans), lambda k, h: (0, k * slabs + j, h[0]))
    return pl.pallas_call(
        functools.partial(vocab_share_body, slabs=slabs, steps=steps, squares=squares),
        grid_spec=pltpu.PrefetchScalarGridSpec(
            num_scalar_prefetch=1,
            grid=(steps,),
            in_specs=[pl.BlockSpec((feats,), lambda k, h: (0,))]
            + [emb_spec(j) for j in range(slabs)]
            + [w_spec(j) for j in range(slabs)]
            + extra_specs,
            out_specs=[whole(*a.shape) for a in out_shape],
            scratch_shapes=scratch,
        ),
        out_shape=out_shape,
        compiler_params=pltpu.CompilerParams(vmem_limit_bytes=60 * MIB),
        name="vocab_share",
    )(half, norm_gain, *([embed_table] * slabs), *([w_streams] * slabs), *extra)


def mixer_body(
    place_ref, tok_ref, own_ref, got_ref, sq_ref, taps_ref, filt_ref, *refs,
    feature_count, chunk,
):
    home, *near, far = refs[:-7]
    vocab_t, toeplitz, tap_cols, carry, prod, gate, conv = refs[-7:]
    chans = far.shape[-1]
    vocab = vocab_t.shape[1]
    blocks = tok_ref.shape[0]
    groups, taps = filt_ref.shape
    gsz = chans // groups
    length = blocks * taps
    genome = pl.program_id(0)

    @pl.when(genome == 0)
    def _():
        sums = (own_ref[...] + got_ref[:vocab].astype(jnp.float32)).T
        tails = []
        for i in range(vocab // LANES):
            at = vocab + (i // 2) * SQ_ROWS
            tail = got_ref[at : at + SQ_ROWS, (i % 2) * LANES : (i % 2 + 1) * LANES]
            tail = tail.astype(jnp.float32)
            tails.append(tail[0:1] + tail[1:2] + tail[2:3])
        squares = sq_ref[...] + jnp.concatenate(tails, axis=1)
        scale = lax.rsqrt(squares / feature_count + 1e-06)
        vocab_t[...] = (sums * scale).astype(jnp.bfloat16)
        row = lax.broadcasted_iota(jnp.int32, (taps, taps), 0)
        col = lax.broadcasted_iota(jnp.int32, (taps, taps), 1)
        filt = filt_ref[...].astype(jnp.float32)
        for g in range(groups):
            circ = pltpu.roll(
                jnp.broadcast_to(filt[g : g + 1], (taps, taps)), 0, 1, stride=1, stride_axis=0
            )
            toeplitz[g, :taps] = jnp.where(col < row, circ, 0.0).astype(jnp.bfloat16)
            toeplitz[g, taps:] = jnp.where(col >= row, circ, 0.0).astype(jnp.bfloat16)
        cols = taps_ref[...].T
        for i in range(9):
            tap_cols[i] = jnp.broadcast_to(cols[:, i : i + 1], (chans, LANES))
        prod[:, :gsz, :] = jnp.zeros((groups, gsz, taps), jnp.bfloat16)

    for k in range(2):
        carry[k] = jnp.zeros(carry.shape[1:], jnp.float32)

    ids = lax.broadcasted_iota(jnp.int32, (vocab, chunk), 0)
    lane = lax.broadcasted_iota(jnp.int32, (chans, LANES), 1)
    per = chunk // taps
    for n in range(length // chunk):
        toks = jnp.concatenate(
            [tok_ref[n * per + b, pl.ds(genome, 1), :] for b in range(per)], axis=1
        )
        picks = jnp.where(ids == toks, 1.0, 0.0)
        proj = jnp.dot(vocab_t[...], picks.astype(jnp.bfloat16), preferred_element_type=jnp.float32)
        mixed = []
        for s in range(3):
            cur = proj[s * chans : (s + 1) * chans]
            wide = lambda i: jnp.concatenate([tap_cols[i]] * per, axis=1)
            total = wide(s) * cur
            backs = []
            for k in (1, 2):
                tiles = []
                before = carry[k - 1, s]
                for b in range(per):
                    turned = pltpu.roll(cur[:, b * LANES : (b + 1) * LANES], k, 1)
                    tiles.append(jnp.where(lane < k, before, turned))
                    before = turned
                carry[k - 1, s] = before
                backs.append(jnp.concatenate(tiles, axis=1))
                total = total + wide(3 * k + s) * backs[-1]
            mixed.append(total)
        inner = (mixed[0] * mixed[2]).astype(jnp.bfloat16)
        for b in range(per):
            gate[n * per + b] = mixed[1][:, b * taps : (b + 1) * taps]
            at = (n * per + b + 1) * gsz
            for g in range(groups):
                prod[g, at : at + gsz, :] = inner[g * gsz : (g + 1) * gsz, b * taps : (b + 1) * taps]
    rows = blocks * gsz
    for g in range(groups):
        pair = jnp.concatenate([prod[g, :rows], prod[g, gsz : gsz + rows]], axis=1)
        conv[g] = jnp.dot(pair, toeplitz[g], preferred_element_type=jnp.float32)
    for r in range(blocks):
        b = place_ref[0] ^ r
        at = pl.ds(pl.multiple_of(b * gsz, gsz), gsz)
        filtered = jnp.concatenate([conv[g, at, :] for g in range(groups)], axis=0)
        gated = (gate[b] * filtered).astype(jnp.bfloat16).T
        k, dx, dc = r >> 2, (r >> 1) & 1, r & 1
        if k == 0:
            home[dx, dc, 0] = gated
        elif dx == 1:
            far[k - 1, dc, 0] = gated
        else:
            near[k - 1][dc, 0] = gated


def mixer(place, tokens, own, got, squares, taps_rows, filt, feature_count):
    blocks, genomes, taps = tokens.shape
    vocab, width = own.shape
    chans = width // 3
    groups, _ = filt.shape
    gsz = chans // groups
    hops = blocks // 4
    length = blocks * taps
    whole = lambda *shape: pl.BlockSpec(shape, lambda g, p: (0,) * len(shape))
    near_shape = (2, genomes, taps, chans)
    packs = lambda n: pl.BlockSpec((n, 2, 1, taps, chans), lambda g, p: (0, 0, g, 0, 0))
    return pl.pallas_call(
        functools.partial(mixer_body, feature_count=feature_count, chunk=4 * taps),
        grid_spec=pltpu.PrefetchScalarGridSpec(
            num_scalar_prefetch=1,
            grid=(genomes,),
            in_specs=[
                whole(blocks, genomes, taps),
                whole(vocab, width),
                whole(*got.shape),
                whole(1, vocab),
                whole(*taps_rows.shape),
                whole(groups, taps),
            ],
            out_specs=[packs(2)]
            + [pl.BlockSpec((2, 1, taps, chans), lambda g, p: (0, g, 0, 0))] * (hops - 1)
            + [packs(hops - 1)],
            scratch_shapes=[
                pltpu.VMEM((width, vocab), jnp.bfloat16),
                pltpu.VMEM((groups, 2 * taps, taps), jnp.bfloat16),
                pltpu.VMEM((9, chans, LANES), jnp.float32),
                pltpu.VMEM((2, 3, chans, LANES), jnp.float32),
                pltpu.VMEM((groups, (blocks + 1) * gsz, taps), jnp.bfloat16),
                pltpu.VMEM((blocks, chans, taps), jnp.float32),
                pltpu.VMEM((groups, blocks * gsz, taps), jnp.float32),
            ],
        ),
        out_shape=[jax.ShapeDtypeStruct((2,) + near_shape, jnp.bfloat16)]
        + [jax.ShapeDtypeStruct(near_shape, jnp.bfloat16)] * (hops - 1)
        + [jax.ShapeDtypeStruct((hops - 1,) + near_shape, jnp.bfloat16)],
        compiler_params=pltpu.CompilerParams(vmem_limit_bytes=26 * MIB),
        cost_estimate=pl.CostEstimate(
            flops=2 * genomes * length * vocab * width,
            bytes_accessed=6 * vocab * width + 2 * genomes * length * chans,
            transcendentals=0,
        ),
        name="mixer",
    )(place, tokens, own, got, squares, taps_rows, filt)


def project_body(place_ref, *refs, columns, first, last, tile):
    hops = len(columns)
    mine, other, cross, w_hbm = refs[:hops], refs[hops : 2 * hops], refs[2 * hops], refs[2 * hops + 1]
    rest = refs[2 * hops + 2 :]
    if first:
        tok_ref, table_ref, out_ref, gated, slabs, arrivals, picks = rest
    elif last:
        acc_ref, out_ref, gated, slabs, arrivals, ready, leaving = rest
    else:
        acc_ref, out_ref, gated, slabs, arrivals = rest
    chans = cross.shape[-1]
    genomes, rows = cross.shape[1:3]
    wide = 4 * chans
    tiles = w_hbm.shape[0] // tile
    arriving = []
    for t in range(tiles):
        for j, c in enumerate(columns):
            at = pl.multiple_of(((place_ref[0] >> 1) ^ c) * wide, wide)
            copy = pltpu.make_async_copy(
                w_hbm.at[pl.ds(t * tile, tile), pl.ds(at, wide)],
                slabs.at[t, :, pl.ds(j * wide, wide)],
                arrivals.at[t, j],
            )
            copy.start()
            arriving.append(copy)

    core, plane = place_ref[0] & 1, place_ref[1]
    for j in range(hops):
        pieces = (
            (mine[j], 0, core, plane),
            (other[j], 0, core, 1 - plane),
            (cross, j, 1 - core, plane),
            (cross, hops + j, 1 - core, 1 - plane),
        )
        for ref, lead, from_core, from_plane in pieces:
            at = j * wide + (2 * from_core + from_plane) * chans
            lanes = pl.ds(pl.multiple_of(at, LANES), chans)
            for g in range(genomes):
                gated[g * rows : (g + 1) * rows, lanes] = ref[lead, g]
    if first:
        vocab = table_ref.shape[0]
        toks = tok_ref[place_ref[0]]
        toks = jnp.concatenate([toks[g : g + 1] for g in range(genomes)], axis=1)
        ids = lax.broadcasted_iota(jnp.int32, (vocab, genomes * rows), 0)
        picks[...] = jnp.where(ids == toks, 1.0, 0.0).T.astype(jnp.bfloat16)

    sending = []
    for t in range(tiles):
        at = slice(t * tile, (t + 1) * tile)
        for j in range(hops):
            arriving[t * hops + j].wait()
        total = lax.dot_general(
            gated[...], slabs[t], (((1,), (1,)), ((), ())), preferred_element_type=jnp.float32
        )
        if first:
            total = total + jnp.dot(
                picks[...], table_ref[:, at], preferred_element_type=jnp.float32
            )
        for g in range(genomes):
            part = total[g * rows : (g + 1) * rows]
            if not first:
                part = part + acc_ref[g, :, at]
            if last:
                ready[g, :, at] = part.astype(ready.dtype)
            else:
                out_ref[g, :, at] = part
        if last:
            copy = pltpu.make_async_copy(ready.at[:, :, at], out_ref.at[:, :, at], leaving.at[t])
            copy.start()
            sending.append(copy)
    for copy in sending:
        copy.wait()


def project(place, mine, other, cross, columns, w_out, start, last=False):
    hops = len(mine)
    first = isinstance(start, tuple)
    _, genomes, rows, chans = cross.shape
    feats = w_out.shape[0]
    tile = 1024
    tiles = feats // tile
    vmem = pl.BlockSpec(memory_space=pltpu.VMEM)
    anywhere = pl.BlockSpec(memory_space=pl.ANY)
    operands = mine + other + [cross, w_out]
    in_specs = [pl.BlockSpec(memory_space=pltpu.SMEM)] + [vmem] * (2 * hops + 1) + [anywhere]
    scratch = [
        pltpu.VMEM((genomes * rows, hops * 4 * chans), jnp.bfloat16),
        pltpu.VMEM((tiles, tile, hops * 4 * chans), jnp.bfloat16),
        pltpu.SemaphoreType.DMA((tiles, hops)),
    ]
    if first:
        operands += list(start)
        in_specs += [vmem, vmem]
        scratch.append(pltpu.VMEM((genomes * rows, start[1].shape[0]), jnp.bfloat16))
    else:
        operands.append(start)
        in_specs.append(vmem)
    shape = (genomes, rows, feats)
    if last:
        scratch += [pltpu.VMEM(shape, jnp.bfloat16), pltpu.SemaphoreType.DMA((tiles,))]
    return pl.pallas_call(
        functools.partial(project_body, columns=columns, first=first, last=last, tile=tile),
        in_specs=in_specs,
        out_specs=anywhere if last else vmem,
        scratch_shapes=scratch,
        out_shape=jax.ShapeDtypeStruct(shape, jnp.bfloat16 if last else jnp.float32),
        compiler_params=pltpu.CompilerParams(vmem_limit_bytes=40 * MIB),
        cost_estimate=pl.CostEstimate(
            flops=2 * genomes * rows * feats * hops * 4 * chans,
            bytes_accessed=2 * feats * hops * 4 * chans + 6 * genomes * rows * feats,
            transcendentals=0,
        ),
        name="project",
    )(place, *operands)


def swap_wt(shard):
    return lax.ppermute(shard, "wt", [(0, 1), (1, 0)])


def swap_seq(shard, step):
    return lax.ppermute(shard, "seq", [(i, i ^ step) for i in range(lax.axis_size("seq"))])


def swap_core(mine, other):
    return swap_seq(jnp.stack([a[1] for a in mine + other]), 1)


def shared_block(tokens, embed_table, norm_gain, w_in, short_taps, filters, w_out):
    me = lax.axis_index("wt")
    local_chans = w_in.shape[2]
    chans = local_chans // 2
    groups = filters.shape[0] // 2
    feature_count = embed_table.shape[1] * lax.axis_size("wt")
    w_streams = jnp.transpose(w_in, (1, 0, 2))
    place = jnp.stack([lax.axis_index("seq"), me]).astype(jnp.int32)
    pick = lambda which: jnp.reshape(which, (1,)).astype(jnp.int32)
    seqs, planes = lax.axis_size("seq"), lax.axis_size("wt")
    sent, squares, copies = vocab_share(
        pick(1 - me), embed_table, norm_gain, w_streams, jnp.bfloat16, tokens, seqs * planes
    )
    got = swap_wt(sent)
    all_tokens = lax.all_to_all(copies, ("seq", "wt"), 0, 0, tiled=True)
    all_tokens = all_tokens.reshape(seqs, planes, tokens.shape[1])
    (own,) = vocab_share(pick(me), embed_table, norm_gain, w_streams, jnp.float32)
    taps_rows = lax.dynamic_slice_in_dim(
        short_taps.astype(jnp.float32).reshape(9, local_chans), me * chans, chans, 1
    )
    taps_rows = jnp.pad(taps_rows, ((0, 7), (0, 0)))
    filt = lax.dynamic_slice_in_dim(filters, me * groups, groups, 0)
    home, *near, far = mixer(
        place, all_tokens, own, got, squares, taps_rows, filt, feature_count
    )
    hops = len(near) + 1
    order = sorted(range(1, hops), key=lambda k: (k == 1, k))
    bar = lax.optimization_barrier
    arrived = swap_seq(far, 2)
    home_other = swap_wt(home)
    near_mine = {k: swap_seq(near[k - 1], 4 * k) for k in order}
    far_mine = {k: swap_seq(arrived[k - 1], 4 * k) for k in order}
    crossed = swap_seq(jnp.stack([home[1], home_other[1]]), 2)
    first_mine, first_other = [home[0]], [home_other[0]]
    cross = swap_core(first_mine, first_other)
    total = project(
        place, first_mine, first_other, cross, [0], w_out, (all_tokens, embed_table)
    )
    near_mine = [near_mine[k] for k in range(1, hops)]
    near_other = swap_wt(jnp.stack(near_mine))
    near_mine = [crossed[0]] + near_mine
    near_other = [crossed[1]] + [near_other[k] for k in range(hops - 1)]
    cross = swap_core(near_mine, near_other)
    far_mine = [far_mine[k] for k in range(1, hops)]
    far_mine, cross = bar((far_mine, cross))
    far_other = swap_wt(jnp.stack(far_mine))
    columns = [1] + [2 * k for k in range(1, hops)]
    total, _ = bar((total, far_mine))
    total = project(place, near_mine, near_other, cross, columns, w_out, total)
    far_other, total = bar((far_other, total))
    far_other = [far_other[k] for k in range(hops - 1)]
    cross = swap_core(far_mine, far_other)
    columns = [2 * k + 1 for k in range(1, hops)]
    return project(place, far_mine, far_other, cross, columns, w_out, total, True)


def local(*args):
    tokens, embed_table, norm_gain, w_in, short_taps, filters, w_out = args
    ranks = lax.axis_size("seq")
    wide = lax.axis_size("wt") == 2 and w_in.shape[2] == 2 * LANES and ranks in (8, 16, 32)
    aligned = tokens.shape[1] == filters.shape[1] == LANES and w_out.shape[0] % 1024 == 0
    if wide and aligned and tokens.shape[0] == 1:
        return shared_block(*args)
    return plain_block(*args)


def solution(mesh):
    placed = (
        P("wt", "seq"),
        P(None, "wt"),
        P("wt"),
        P("wt", None, "seq"),
        P(None, None, "seq"),
        P("seq", None),
        P("wt", None),
    )
    return jax.shard_map(
        local, mesh=mesh, in_specs=placed, out_specs=P(None, "seq", "wt"), check_vma=False
    )
```

```python
import functools

import jax
import jax.numpy as jnp
from jax import lax
from jax.experimental import pallas as pl
from jax.experimental.pallas import tpu as pltpu
from jax.sharding import PartitionSpec as P

LANES = 128
SQ_ROWS = 16
MIB = 1 << 20


def shifted(shard, axis, by):
    size = lax.axis_size(axis)
    pairs = [(i, i + by) for i in range(size) if 0 <= i + by < size]
    return lax.ppermute(shard, axis, pairs)


def causal_pair(filter_vals):
    tap_count = filter_vals.shape[1]
    group_count = filter_vals.shape[0]
    tiled_taps = jnp.tile(filter_vals, (1, 2 * tap_count - 1)).reshape(
        group_count, tap_count, 2 * tap_count - 1
    )[:, :, :tap_count]
    circulant = jnp.swapaxes(tiled_taps, 1, 2)
    row_pos = lax.broadcasted_iota(jnp.int32, (tap_count, tap_count), 0)
    col_pos = lax.broadcasted_iota(jnp.int32, (tap_count, tap_count), 1)
    lower_mask = (row_pos >= col_pos)[None]
    zero_mat = jnp.zeros_like(circulant)
    return (jnp.where(lower_mask, circulant, zero_mat), jnp.where(lower_mask, zero_mat, circulant))


def short_mix(extended, tap_vals):
    row_count = extended.shape[0] - 2
    ext_vals = extended.astype(jnp.float32)
    return (
        tap_vals[0] * ext_vals[2 : 2 + row_count]
        + tap_vals[1] * ext_vals[1 : 1 + row_count]
        + tap_vals[2] * ext_vals[0:row_count]
    )


def run_filter(extended, lower_mat, upper_mat):
    tap_count = lower_mat.shape[1]
    group_count = lower_mat.shape[0]
    chan_count = extended.shape[1]
    blocks = extended.shape[0] // tap_count
    stacked = extended.reshape(blocks, tap_count, group_count, chan_count // group_count)
    filtered = jnp.einsum(
        "gij,bjgc->bigc", lower_mat, stacked[1:], preferred_element_type=jnp.float32
    )
    filtered = filtered + jnp.einsum(
        "gij,bjgc->bigc", upper_mat, stacked[:-1], preferred_element_type=jnp.float32
    )
    return filtered.reshape((blocks - 1) * tap_count, chan_count)


def plain_block(tokens, embed_table, norm_gain, w_in, short_taps, filters, w_out):
    token_ids = tokens[0]
    own_len = token_ids.shape[0]
    tap_count = filters.shape[1]
    table_vals = embed_table.astype(jnp.float32)
    square_sums = lax.psum(jnp.sum(table_vals * table_vals, axis=1, keepdims=True), "wt")
    feature_count = embed_table.shape[1] * lax.axis_size("wt")
    row_scale = lax.rsqrt(square_sums / feature_count + 1e-06)
    normed = (table_vals * row_scale * norm_gain.astype(jnp.float32)).astype(jnp.bfloat16)
    local_chans = w_in.shape[2]
    w_flat = w_in.reshape(w_in.shape[0], 3 * local_chans)
    vocab_size = embed_table.shape[0]
    partial_sum = jnp.dot(normed, w_flat, preferred_element_type=jnp.float32)
    vocab_flat = lax.psum(partial_sum, "wt").astype(jnp.bfloat16)
    vocab_proj = vocab_flat.reshape(vocab_size, 3, local_chans)
    vocab_all, tap_all, filter_all = (
        lax.all_gather(vocab_proj, "seq", axis=2, tiled=True),
        lax.all_gather(short_taps, "seq", axis=2, tiled=True),
        lax.all_gather(filters, "seq", axis=0, tiled=True),
    )
    projected = jnp.take(vocab_all, token_ids, axis=0)
    edge_prev = shifted(projected[own_len - 2 :], "seq", 1)
    mixture = short_mix(
        jnp.concatenate([edge_prev, projected], axis=0), tap_all.astype(jnp.float32)
    )
    product = (mixture[:, 0] * mixture[:, 2]).astype(jnp.bfloat16)
    tail_prev = shifted(product[own_len - tap_count + 1 :], "seq", 1)
    chan_count = product.shape[1]
    extended = jnp.concatenate(
        [jnp.zeros((1, chan_count), jnp.bfloat16), tail_prev, product], axis=0
    )
    lower_mat, upper_mat = causal_pair(filter_all)
    filtered = run_filter(extended, lower_mat, upper_mat)
    gated = (mixture[:, 1] * filtered).astype(jnp.bfloat16)
    everyone = lax.all_gather(tokens, "wt", axis=0, tiled=True)
    branch = jnp.einsum(
        "knc,dc->knd",
        lax.all_gather(gated[None], "wt", axis=0, tiled=True),
        w_out,
        preferred_element_type=jnp.float32,
    )
    embedded = jnp.take(embed_table, everyone, axis=0)
    return (embedded.astype(jnp.float32) + branch).astype(jnp.bfloat16)


def three_parts(vals):
    parts = []
    for _ in range(3):
        parts.append(vals.astype(jnp.bfloat16).astype(jnp.float32))
        vals = vals - parts[-1]
    return parts


def vocab_share_body(half_ref, gain_ref, *refs, slabs, steps, squares):
    embs, weights = refs[:slabs], refs[slabs : 2 * slabs]
    if squares:
        tok_ref, out_ref, sq_ref, copies_ref, acc_ref, sq_acc = refs[2 * slabs :]
    else:
        out_ref, acc_ref = refs[2 * slabs :]
    step = pl.program_id(0)
    depth = embs[0].shape[1]
    term = part = None
    for j in range(slabs):
        emb = embs[j][...]
        at = pl.multiple_of((step * slabs + j) * depth, LANES)
        scaled = emb * gain_ref[pl.ds(at, depth)][None]
        wide = jnp.concatenate([weights[j][s] for s in range(weights[j].shape[0])], axis=1)
        more = jnp.dot(scaled, wide, preferred_element_type=jnp.float32)
        term = more if term is None else term + more
        if squares:
            vals = emb.astype(jnp.float32)
            vals = vals * vals
            for i in range(depth // LANES):
                piece = vals[:, i * LANES : (i + 1) * LANES]
                part = piece if part is None else part + piece

    @pl.when(step == 0)
    def _():
        acc_ref[...] = term
        if squares:
            sq_acc[...] = part

    @pl.when(step > 0)
    def _():
        acc_ref[...] += term
        if squares:
            sq_acc[...] += part

    @pl.when(step == steps - 1)
    def _():
        vocab = acc_ref.shape[0]
        out_ref[:vocab] = acc_ref[...].astype(out_ref.dtype)
        if squares:
            sums = jnp.sum(sq_acc[...].T, axis=0, keepdims=True)
            sq_ref[...] = sums
            tail = jnp.zeros((SQ_ROWS, vocab), jnp.float32)
            row = lax.broadcasted_iota(jnp.int32, tail.shape, 0)
            for i, piece in enumerate(three_parts(sums)):
                tail = jnp.where(row == i, piece, tail)
            for i in range(vocab // LANES):
                at = vocab + (i // 2) * SQ_ROWS
                out_ref[at : at + SQ_ROWS, (i % 2) * LANES : (i % 2 + 1) * LANES] = tail[
                    :, i * LANES : (i + 1) * LANES
                ].astype(out_ref.dtype)
            copies_ref[...] = jnp.broadcast_to(tok_ref[...][None], copies_ref.shape)


def vocab_share(half, embed_table, norm_gain, w_streams, out_dtype, tokens=None, ranks=0):
    squares = tokens is not None
    vocab, feats = embed_table.shape
    streams, _, local_chans = w_streams.shape
    chans = local_chans // 2
    slabs, steps = 2, 2
    depth = feats // (slabs * steps)
    width = streams * chans
    whole = lambda *shape: pl.BlockSpec(shape, lambda k, h: (0,) * len(shape))
    rows = vocab + (SQ_ROWS * vocab // (2 * LANES) if squares else 0)
    out_shape = [jax.ShapeDtypeStruct((rows, width), out_dtype)]
    scratch = [pltpu.VMEM((vocab, width), jnp.float32)]
    extra_specs, extra = [], []
    if squares:
        extra_specs, extra = [whole(*tokens.shape)], [tokens]
        out_shape.append(jax.ShapeDtypeStruct((1, vocab), jnp.float32))
        out_shape.append(jax.ShapeDtypeStruct((ranks,) + tokens.shape, tokens.dtype))
        scratch.append(pltpu.VMEM((vocab, LANES), jnp.float32))
    emb_spec = lambda j: pl.BlockSpec((vocab, depth), lambda k, h: (0, k * slabs + j))
    w_spec = lambda j: pl.BlockSpec((streams, depth, chans), lambda k, h: (0, k * slabs + j, h[0]))
    return pl.pallas_call(
        functools.partial(vocab_share_body, slabs=slabs, steps=steps, squares=squares),
        grid_spec=pltpu.PrefetchScalarGridSpec(
            num_scalar_prefetch=1,
            grid=(steps,),
            in_specs=[pl.BlockSpec((feats,), lambda k, h: (0,))]
            + [emb_spec(j) for j in range(slabs)]
            + [w_spec(j) for j in range(slabs)]
            + extra_specs,
            out_specs=[whole(*a.shape) for a in out_shape],
            scratch_shapes=scratch,
        ),
        out_shape=out_shape,
        compiler_params=pltpu.CompilerParams(vmem_limit_bytes=60 * MIB),
        name="vocab_share",
    )(half, norm_gain, *([embed_table] * slabs), *([w_streams] * slabs), *extra)


def mixer_body(
    place_ref, tok_ref, own_ref, got_ref, sq_ref, taps_ref, filt_ref, *refs,
    feature_count, chunk,
):
    home, *near, far = refs[:-7]
    vocab_t, toeplitz, tap_cols, carry, prod, gate, conv = refs[-7:]
    chans = far.shape[-1]
    vocab = vocab_t.shape[1]
    blocks = tok_ref.shape[0]
    groups, taps = filt_ref.shape
    gsz = chans // groups
    length = blocks * taps
    genome = pl.program_id(0)

    @pl.when(genome == 0)
    def _():
        sums = (own_ref[...] + got_ref[:vocab].astype(jnp.float32)).T
        tails = []
        for i in range(vocab // LANES):
            at = vocab + (i // 2) * SQ_ROWS
            tail = got_ref[at : at + SQ_ROWS, (i % 2) * LANES : (i % 2 + 1) * LANES]
            tail = tail.astype(jnp.float32)
            tails.append(tail[0:1] + tail[1:2] + tail[2:3])
        squares = sq_ref[...] + jnp.concatenate(tails, axis=1)
        scale = lax.rsqrt(squares / feature_count + 1e-06)
        vocab_t[...] = (sums * scale).astype(jnp.bfloat16)
        row = lax.broadcasted_iota(jnp.int32, (taps, taps), 0)
        col = lax.broadcasted_iota(jnp.int32, (taps, taps), 1)
        filt = filt_ref[...].astype(jnp.float32)
        for g in range(groups):
            circ = pltpu.roll(
                jnp.broadcast_to(filt[g : g + 1], (taps, taps)), 0, 1, stride=1, stride_axis=0
            )
            toeplitz[g, :taps] = jnp.where(col < row, circ, 0.0).astype(jnp.bfloat16)
            toeplitz[g, taps:] = jnp.where(col >= row, circ, 0.0).astype(jnp.bfloat16)
        cols = taps_ref[...].T
        for i in range(9):
            tap_cols[i] = jnp.broadcast_to(cols[:, i : i + 1], (chans, LANES))
        prod[:, :gsz, :] = jnp.zeros((groups, gsz, taps), jnp.bfloat16)

    for k in range(2):
        carry[k] = jnp.zeros(carry.shape[1:], jnp.float32)

    ids = lax.broadcasted_iota(jnp.int32, (vocab, chunk), 0).astype(jnp.int16)
    one, zero = jnp.ones((), jnp.bfloat16), jnp.zeros((), jnp.bfloat16)
    lane = lax.broadcasted_iota(jnp.int32, (chans, LANES), 1)
    per = chunk // taps
    for n in range(length // chunk):
        toks = jnp.concatenate(
            [tok_ref[n * per + b, pl.ds(genome, 1), :] for b in range(per)], axis=1
        )
        picks = jnp.where(ids == toks.astype(jnp.int16), one, zero)
        proj = jnp.dot(vocab_t[...], picks, preferred_element_type=jnp.float32)
        mixed = []
        for s in range(3):
            cur = proj[s * chans : (s + 1) * chans]
            wide = lambda i: jnp.concatenate([tap_cols[i]] * per, axis=1)
            total = wide(s) * cur
            backs = []
            for k in (1, 2):
                tiles = []
                before = carry[k - 1, s]
                for b in range(per):
                    turned = pltpu.roll(cur[:, b * LANES : (b + 1) * LANES], k, 1)
                    tiles.append(jnp.where(lane < k, before, turned))
                    before = turned
                carry[k - 1, s] = before
                backs.append(jnp.concatenate(tiles, axis=1))
                total = total + wide(3 * k + s) * backs[-1]
            mixed.append(total)
        inner = (mixed[0] * mixed[2]).astype(jnp.bfloat16)
        for b in range(per):
            gate[n * per + b] = mixed[1][:, b * taps : (b + 1) * taps]
            at = (n * per + b + 1) * gsz
            for g in range(groups):
                prod[g, at : at + gsz, :] = inner[g * gsz : (g + 1) * gsz, b * taps : (b + 1) * taps]
    rows = blocks * gsz
    for g in range(groups):
        pair = jnp.concatenate([prod[g, :rows], prod[g, gsz : gsz + rows]], axis=1)
        conv[g] = jnp.dot(pair, toeplitz[g], preferred_element_type=jnp.float32)
    for r in range(blocks):
        b = place_ref[0] ^ r
        at = pl.ds(pl.multiple_of(b * gsz, gsz), gsz)
        filtered = jnp.concatenate([conv[g, at, :] for g in range(groups)], axis=0)
        gated = (gate[b] * filtered).astype(jnp.bfloat16).T
        k, dx, dc = r >> 2, (r >> 1) & 1, r & 1
        if k == 0:
            home[dx, dc, 0] = gated
        elif dx == 1:
            far[k - 1, dc, 0] = gated
        else:
            near[k - 1][dc, 0] = gated


def mixer(place, tokens, own, got, squares, taps_rows, filt, feature_count):
    blocks, genomes, taps = tokens.shape
    vocab, width = own.shape
    chans = width // 3
    groups, _ = filt.shape
    gsz = chans // groups
    hops = blocks // 4
    length = blocks * taps
    whole = lambda *shape: pl.BlockSpec(shape, lambda g, p: (0,) * len(shape))
    near_shape = (2, genomes, taps, chans)
    packs = lambda n: pl.BlockSpec((n, 2, 1, taps, chans), lambda g, p: (0, 0, g, 0, 0))
    return pl.pallas_call(
        functools.partial(mixer_body, feature_count=feature_count, chunk=4 * taps),
        grid_spec=pltpu.PrefetchScalarGridSpec(
            num_scalar_prefetch=1,
            grid=(genomes,),
            in_specs=[
                whole(blocks, genomes, taps),
                whole(vocab, width),
                whole(*got.shape),
                whole(1, vocab),
                whole(*taps_rows.shape),
                whole(groups, taps),
            ],
            out_specs=[packs(2)]
            + [pl.BlockSpec((2, 1, taps, chans), lambda g, p: (0, g, 0, 0))] * (hops - 1)
            + [packs(hops - 1)],
            scratch_shapes=[
                pltpu.VMEM((width, vocab), jnp.bfloat16),
                pltpu.VMEM((groups, 2 * taps, taps), jnp.bfloat16),
                pltpu.VMEM((9, chans, LANES), jnp.float32),
                pltpu.VMEM((2, 3, chans, LANES), jnp.float32),
                pltpu.VMEM((groups, (blocks + 1) * gsz, taps), jnp.bfloat16),
                pltpu.VMEM((blocks, chans, taps), jnp.float32),
                pltpu.VMEM((groups, blocks * gsz, taps), jnp.float32),
            ],
        ),
        out_shape=[jax.ShapeDtypeStruct((2,) + near_shape, jnp.bfloat16)]
        + [jax.ShapeDtypeStruct(near_shape, jnp.bfloat16)] * (hops - 1)
        + [jax.ShapeDtypeStruct((hops - 1,) + near_shape, jnp.bfloat16)],
        compiler_params=pltpu.CompilerParams(vmem_limit_bytes=26 * MIB),
        cost_estimate=pl.CostEstimate(
            flops=2 * genomes * length * vocab * width,
            bytes_accessed=6 * vocab * width + 2 * genomes * length * chans,
            transcendentals=0,
        ),
        name="mixer",
    )(place, tokens, own, got, squares, taps_rows, filt)


def project_body(place_ref, *refs, columns, first, last, tile):
    hops = len(columns)
    mine, other, cross, w_hbm = refs[:hops], refs[hops : 2 * hops], refs[2 * hops], refs[2 * hops + 1]
    rest = refs[2 * hops + 2 :]
    if first:
        tok_ref, table_ref, out_ref, gated, slabs, arrivals, picks = rest
    elif last:
        acc_ref, out_ref, gated, slabs, arrivals, ready, leaving = rest
    else:
        acc_ref, out_ref, gated, slabs, arrivals = rest
    chans = cross.shape[-1]
    genomes, rows = cross.shape[1:3]
    wide = 4 * chans
    tiles = w_hbm.shape[0] // tile
    arriving = []
    for t in range(tiles):
        for j, c in enumerate(columns):
            at = pl.multiple_of(((place_ref[0] >> 1) ^ c) * wide, wide)
            copy = pltpu.make_async_copy(
                w_hbm.at[pl.ds(t * tile, tile), pl.ds(at, wide)],
                slabs.at[t, :, pl.ds(j * wide, wide)],
                arrivals.at[t, j],
            )
            copy.start()
            arriving.append(copy)

    core, plane = place_ref[0] & 1, place_ref[1]
    for j in range(hops):
        pieces = (
            (mine[j], 0, core, plane),
            (other[j], 0, core, 1 - plane),
            (cross, j, 1 - core, plane),
            (cross, hops + j, 1 - core, 1 - plane),
        )
        for ref, lead, from_core, from_plane in pieces:
            at = j * wide + (2 * from_core + from_plane) * chans
            lanes = pl.ds(pl.multiple_of(at, LANES), chans)
            for g in range(genomes):
                gated[g * rows : (g + 1) * rows, lanes] = ref[lead, g]
    if first:
        vocab = table_ref.shape[0]
        toks = tok_ref[place_ref[0]]
        toks = jnp.concatenate([toks[g : g + 1] for g in range(genomes)], axis=1)
        ids = lax.broadcasted_iota(jnp.int32, (vocab, genomes * rows), 0)
        picks[...] = jnp.where(ids == toks, 1.0, 0.0).T.astype(jnp.bfloat16)

    sending = []
    for t in range(tiles):
        at = slice(t * tile, (t + 1) * tile)
        for j in range(hops):
            arriving[t * hops + j].wait()
        total = lax.dot_general(
            gated[...], slabs[t], (((1,), (1,)), ((), ())), preferred_element_type=jnp.float32
        )
        if first:
            total = total + jnp.dot(
                picks[...], table_ref[:, at], preferred_element_type=jnp.float32
            )
        for g in range(genomes):
            part = total[g * rows : (g + 1) * rows]
            if not first:
                part = part + acc_ref[g, :, at]
            if last:
                ready[g, :, at] = part.astype(ready.dtype)
            else:
                out_ref[g, :, at] = part
        if last:
            copy = pltpu.make_async_copy(ready.at[:, :, at], out_ref.at[:, :, at], leaving.at[t])
            copy.start()
            sending.append(copy)
    for copy in sending:
        copy.wait()


def project(place, mine, other, cross, columns, w_out, start, last=False):
    hops = len(mine)
    first = isinstance(start, tuple)
    _, genomes, rows, chans = cross.shape
    feats = w_out.shape[0]
    tile = 1024
    tiles = feats // tile
    vmem = pl.BlockSpec(memory_space=pltpu.VMEM)
    anywhere = pl.BlockSpec(memory_space=pl.ANY)
    operands = mine + other + [cross, w_out]
    in_specs = [pl.BlockSpec(memory_space=pltpu.SMEM)] + [vmem] * (2 * hops + 1) + [anywhere]
    scratch = [
        pltpu.VMEM((genomes * rows, hops * 4 * chans), jnp.bfloat16),
        pltpu.VMEM((tiles, tile, hops * 4 * chans), jnp.bfloat16),
        pltpu.SemaphoreType.DMA((tiles, hops)),
    ]
    if first:
        operands += list(start)
        in_specs += [vmem, vmem]
        scratch.append(pltpu.VMEM((genomes * rows, start[1].shape[0]), jnp.bfloat16))
    else:
        operands.append(start)
        in_specs.append(vmem)
    shape = (genomes, rows, feats)
    if last:
        scratch += [pltpu.VMEM(shape, jnp.bfloat16), pltpu.SemaphoreType.DMA((tiles,))]
    return pl.pallas_call(
        functools.partial(project_body, columns=columns, first=first, last=last, tile=tile),
        in_specs=in_specs,
        out_specs=anywhere if last else vmem,
        scratch_shapes=scratch,
        out_shape=jax.ShapeDtypeStruct(shape, jnp.bfloat16 if last else jnp.float32),
        compiler_params=pltpu.CompilerParams(vmem_limit_bytes=40 * MIB),
        cost_estimate=pl.CostEstimate(
            flops=2 * genomes * rows * feats * hops * 4 * chans,
            bytes_accessed=2 * feats * hops * 4 * chans + 6 * genomes * rows * feats,
            transcendentals=0,
        ),
        name="project",
    )(place, *operands)


def swap_wt(shard):
    return lax.ppermute(shard, "wt", [(0, 1), (1, 0)])


def swap_seq(shard, step):
    return lax.ppermute(shard, "seq", [(i, i ^ step) for i in range(lax.axis_size("seq"))])


def swap_core(mine, other):
    return swap_seq(jnp.stack([a[1] for a in mine + other]), 1)


def shared_block(tokens, embed_table, norm_gain, w_in, short_taps, filters, w_out):
    me = lax.axis_index("wt")
    local_chans = w_in.shape[2]
    chans = local_chans // 2
    groups = filters.shape[0] // 2
    feature_count = embed_table.shape[1] * lax.axis_size("wt")
    w_streams = jnp.transpose(w_in, (1, 0, 2))
    place = jnp.stack([lax.axis_index("seq"), me]).astype(jnp.int32)
    pick = lambda which: jnp.reshape(which, (1,)).astype(jnp.int32)
    seqs, planes = lax.axis_size("seq"), lax.axis_size("wt")
    sent, squares, copies = vocab_share(
        pick(1 - me), embed_table, norm_gain, w_streams, jnp.bfloat16, tokens, seqs * planes
    )
    got = swap_wt(sent)
    all_tokens = lax.all_to_all(copies, ("seq", "wt"), 0, 0, tiled=True)
    all_tokens = all_tokens.reshape(seqs, planes, tokens.shape[1])
    (own,) = vocab_share(pick(me), embed_table, norm_gain, w_streams, jnp.float32)
    taps_rows = lax.dynamic_slice_in_dim(
        short_taps.astype(jnp.float32).reshape(9, local_chans), me * chans, chans, 1
    )
    taps_rows = jnp.pad(taps_rows, ((0, 7), (0, 0)))
    filt = lax.dynamic_slice_in_dim(filters, me * groups, groups, 0)
    home, *near, far = mixer(
        place, all_tokens, own, got, squares, taps_rows, filt, feature_count
    )
    hops = len(near) + 1
    order = sorted(range(1, hops), key=lambda k: (k == 1, k))
    bar = lax.optimization_barrier
    arrived = swap_seq(far, 2)
    home_other = swap_wt(home)
    near_mine = {k: swap_seq(near[k - 1], 4 * k) for k in order}
    arrived, near_mine[1] = bar((arrived, near_mine[1]))
    far_mine = {k: swap_seq(arrived[k - 1], 4 * k) for k in order}
    crossed = swap_seq(jnp.stack([home[1], home_other[1]]), 2)
    first_mine, first_other = [home[0]], [home_other[0]]
    cross = swap_core(first_mine, first_other)
    total = project(
        place, first_mine, first_other, cross, [0], w_out, (all_tokens, embed_table)
    )
    near_mine = [near_mine[k] for k in range(1, hops)]
    near_other = swap_wt(jnp.stack(near_mine))
    near_mine = [crossed[0]] + near_mine
    near_other = [crossed[1]] + [near_other[k] for k in range(hops - 1)]
    cross = swap_core(near_mine, near_other)
    far_mine = [far_mine[k] for k in range(1, hops)]
    far_mine, cross = bar((far_mine, cross))
    far_other = swap_wt(jnp.stack(far_mine))
    columns = [1] + [2 * k for k in range(1, hops)]
    total, _ = bar((total, far_mine))
    total = project(place, near_mine, near_other, cross, columns, w_out, total)
    far_other, total = bar((far_other, total))
    far_other = [far_other[k] for k in range(hops - 1)]
    cross = swap_core(far_mine, far_other)
    columns = [2 * k + 1 for k in range(1, hops)]
    return project(place, far_mine, far_other, cross, columns, w_out, total, True)


def local(*args):
    tokens, embed_table, norm_gain, w_in, short_taps, filters, w_out = args
    ranks = lax.axis_size("seq")
    wide = lax.axis_size("wt") == 2 and w_in.shape[2] == 2 * LANES and ranks in (8, 16, 32)
    aligned = tokens.shape[1] == filters.shape[1] == LANES and w_out.shape[0] % 1024 == 0
    if wide and aligned and tokens.shape[0] == 1:
        return shared_block(*args)
    return plain_block(*args)


def solution(mesh):
    placed = (
        P("wt", "seq"),
        P(None, "wt"),
        P("wt"),
        P("wt", None, "seq"),
        P(None, None, "seq"),
        P("seq", None),
        P("wt", None),
    )
    return jax.shard_map(
        local, mesh=mesh, in_specs=placed, out_specs=P(None, "seq", "wt"), check_vma=False
    )
```

```python
import functools

import jax
import jax.numpy as jnp
from jax import lax
from jax.experimental import pallas as pl
from jax.experimental.pallas import tpu as pltpu
from jax.sharding import PartitionSpec as P

LANES = 128
SQ_ROWS = 16
MIB = 1 << 20


def shifted(shard, axis, by):
    size = lax.axis_size(axis)
    pairs = [(i, i + by) for i in range(size) if 0 <= i + by < size]
    return lax.ppermute(shard, axis, pairs)


def causal_pair(filter_vals):
    tap_count = filter_vals.shape[1]
    group_count = filter_vals.shape[0]
    tiled_taps = jnp.tile(filter_vals, (1, 2 * tap_count - 1)).reshape(
        group_count, tap_count, 2 * tap_count - 1
    )[:, :, :tap_count]
    circulant = jnp.swapaxes(tiled_taps, 1, 2)
    row_pos = lax.broadcasted_iota(jnp.int32, (tap_count, tap_count), 0)
    col_pos = lax.broadcasted_iota(jnp.int32, (tap_count, tap_count), 1)
    lower_mask = (row_pos >= col_pos)[None]
    zero_mat = jnp.zeros_like(circulant)
    return (jnp.where(lower_mask, circulant, zero_mat), jnp.where(lower_mask, zero_mat, circulant))


def short_mix(extended, tap_vals):
    row_count = extended.shape[0] - 2
    ext_vals = extended.astype(jnp.float32)
    return (
        tap_vals[0] * ext_vals[2 : 2 + row_count]
        + tap_vals[1] * ext_vals[1 : 1 + row_count]
        + tap_vals[2] * ext_vals[0:row_count]
    )


def run_filter(extended, lower_mat, upper_mat):
    tap_count = lower_mat.shape[1]
    group_count = lower_mat.shape[0]
    chan_count = extended.shape[1]
    blocks = extended.shape[0] // tap_count
    stacked = extended.reshape(blocks, tap_count, group_count, chan_count // group_count)
    filtered = jnp.einsum(
        "gij,bjgc->bigc", lower_mat, stacked[1:], preferred_element_type=jnp.float32
    )
    filtered = filtered + jnp.einsum(
        "gij,bjgc->bigc", upper_mat, stacked[:-1], preferred_element_type=jnp.float32
    )
    return filtered.reshape((blocks - 1) * tap_count, chan_count)


def plain_block(tokens, embed_table, norm_gain, w_in, short_taps, filters, w_out):
    token_ids = tokens[0]
    own_len = token_ids.shape[0]
    tap_count = filters.shape[1]
    table_vals = embed_table.astype(jnp.float32)
    square_sums = lax.psum(jnp.sum(table_vals * table_vals, axis=1, keepdims=True), "wt")
    feature_count = embed_table.shape[1] * lax.axis_size("wt")
    row_scale = lax.rsqrt(square_sums / feature_count + 1e-06)
    normed = (table_vals * row_scale * norm_gain.astype(jnp.float32)).astype(jnp.bfloat16)
    local_chans = w_in.shape[2]
    w_flat = w_in.reshape(w_in.shape[0], 3 * local_chans)
    vocab_size = embed_table.shape[0]
    partial_sum = jnp.dot(normed, w_flat, preferred_element_type=jnp.float32)
    vocab_flat = lax.psum(partial_sum, "wt").astype(jnp.bfloat16)
    vocab_proj = vocab_flat.reshape(vocab_size, 3, local_chans)
    vocab_all, tap_all, filter_all = (
        lax.all_gather(vocab_proj, "seq", axis=2, tiled=True),
        lax.all_gather(short_taps, "seq", axis=2, tiled=True),
        lax.all_gather(filters, "seq", axis=0, tiled=True),
    )
    projected = jnp.take(vocab_all, token_ids, axis=0)
    edge_prev = shifted(projected[own_len - 2 :], "seq", 1)
    mixture = short_mix(
        jnp.concatenate([edge_prev, projected], axis=0), tap_all.astype(jnp.float32)
    )
    product = (mixture[:, 0] * mixture[:, 2]).astype(jnp.bfloat16)
    tail_prev = shifted(product[own_len - tap_count + 1 :], "seq", 1)
    chan_count = product.shape[1]
    extended = jnp.concatenate(
        [jnp.zeros((1, chan_count), jnp.bfloat16), tail_prev, product], axis=0
    )
    lower_mat, upper_mat = causal_pair(filter_all)
    filtered = run_filter(extended, lower_mat, upper_mat)
    gated = (mixture[:, 1] * filtered).astype(jnp.bfloat16)
    everyone = lax.all_gather(tokens, "wt", axis=0, tiled=True)
    branch = jnp.einsum(
        "knc,dc->knd",
        lax.all_gather(gated[None], "wt", axis=0, tiled=True),
        w_out,
        preferred_element_type=jnp.float32,
    )
    embedded = jnp.take(embed_table, everyone, axis=0)
    return (embedded.astype(jnp.float32) + branch).astype(jnp.bfloat16)


def three_parts(vals):
    parts = []
    for _ in range(3):
        parts.append(vals.astype(jnp.bfloat16).astype(jnp.float32))
        vals = vals - parts[-1]
    return parts


def vocab_share_body(half_ref, gain_ref, *refs, slabs, steps, squares):
    embs, weights = refs[:slabs], refs[slabs : 2 * slabs]
    if squares:
        tok_ref, out_ref, sq_ref, copies_ref, acc_ref, sq_acc = refs[2 * slabs :]
    else:
        out_ref, acc_ref = refs[2 * slabs :]
    step = pl.program_id(0)
    depth = embs[0].shape[1]
    term = part = None
    for j in range(slabs):
        emb = embs[j][...]
        at = pl.multiple_of((step * slabs + j) * depth, LANES)
        scaled = emb * gain_ref[pl.ds(at, depth)][None]
        wide = jnp.concatenate([weights[j][s] for s in range(weights[j].shape[0])], axis=1)
        more = jnp.dot(scaled, wide, preferred_element_type=jnp.float32)
        term = more if term is None else term + more
        if squares:
            vals = emb.astype(jnp.float32)
            vals = vals * vals
            for i in range(depth // LANES):
                piece = vals[:, i * LANES : (i + 1) * LANES]
                part = piece if part is None else part + piece

    @pl.when(step == 0)
    def _():
        acc_ref[...] = term
        if squares:
            sq_acc[...] = part

    @pl.when(step > 0)
    def _():
        acc_ref[...] += term
        if squares:
            sq_acc[...] += part

    @pl.when(step == steps - 1)
    def _():
        vocab = acc_ref.shape[0]
        out_ref[:vocab] = acc_ref[...].astype(out_ref.dtype)
        if squares:
            sums = jnp.sum(sq_acc[...].T, axis=0, keepdims=True)
            sq_ref[...] = sums
            tail = jnp.zeros((SQ_ROWS, vocab), jnp.float32)
            row = lax.broadcasted_iota(jnp.int32, tail.shape, 0)
            for i, piece in enumerate(three_parts(sums)):
                tail = jnp.where(row == i, piece, tail)
            for i in range(vocab // LANES):
                at = vocab + (i // 2) * SQ_ROWS
                out_ref[at : at + SQ_ROWS, (i % 2) * LANES : (i % 2 + 1) * LANES] = tail[
                    :, i * LANES : (i + 1) * LANES
                ].astype(out_ref.dtype)
            copies_ref[...] = jnp.broadcast_to(tok_ref[...][None], copies_ref.shape)


def vocab_share(half, embed_table, norm_gain, w_streams, out_dtype, tokens=None, ranks=0):
    squares = tokens is not None
    vocab, feats = embed_table.shape
    streams, _, local_chans = w_streams.shape
    chans = local_chans // 2
    slabs, steps = 2, 2
    depth = feats // (slabs * steps)
    width = streams * chans
    whole = lambda *shape: pl.BlockSpec(shape, lambda k, h: (0,) * len(shape))
    rows = vocab + (SQ_ROWS * vocab // (2 * LANES) if squares else 0)
    out_shape = [jax.ShapeDtypeStruct((rows, width), out_dtype)]
    scratch = [pltpu.VMEM((vocab, width), jnp.float32)]
    extra_specs, extra = [], []
    if squares:
        extra_specs, extra = [whole(*tokens.shape)], [tokens]
        out_shape.append(jax.ShapeDtypeStruct((1, vocab), jnp.float32))
        out_shape.append(jax.ShapeDtypeStruct((ranks,) + tokens.shape, tokens.dtype))
        scratch.append(pltpu.VMEM((vocab, LANES), jnp.float32))
    emb_spec = lambda j: pl.BlockSpec((vocab, depth), lambda k, h: (0, k * slabs + j))
    w_spec = lambda j: pl.BlockSpec((streams, depth, chans), lambda k, h: (0, k * slabs + j, h[0]))
    return pl.pallas_call(
        functools.partial(vocab_share_body, slabs=slabs, steps=steps, squares=squares),
        grid_spec=pltpu.PrefetchScalarGridSpec(
            num_scalar_prefetch=1,
            grid=(steps,),
            in_specs=[pl.BlockSpec((feats,), lambda k, h: (0,))]
            + [emb_spec(j) for j in range(slabs)]
            + [w_spec(j) for j in range(slabs)]
            + extra_specs,
            out_specs=[whole(*a.shape) for a in out_shape],
            scratch_shapes=scratch,
        ),
        out_shape=out_shape,
        compiler_params=pltpu.CompilerParams(vmem_limit_bytes=60 * MIB),
        name="vocab_share",
    )(half, norm_gain, *([embed_table] * slabs), *([w_streams] * slabs), *extra)


def mixer_body(
    place_ref, tok_ref, own_ref, got_ref, sq_ref, taps_ref, filt_ref, *refs,
    feature_count, chunk,
):
    home, *near, far = refs[:-7]
    vocab_t, toeplitz, tap_cols, carry, prod, gate, conv = refs[-7:]
    chans = far.shape[-1]
    vocab = vocab_t.shape[1]
    blocks = tok_ref.shape[0]
    groups, taps = filt_ref.shape
    gsz = chans // groups
    length = blocks * taps
    genome = pl.program_id(0)

    @pl.when(genome == 0)
    def _():
        sums = (own_ref[...] + got_ref[:vocab].astype(jnp.float32)).T
        tails = []
        for i in range(vocab // LANES):
            at = vocab + (i // 2) * SQ_ROWS
            tail = got_ref[at : at + SQ_ROWS, (i % 2) * LANES : (i % 2 + 1) * LANES]
            tail = tail.astype(jnp.float32)
            tails.append(tail[0:1] + tail[1:2] + tail[2:3])
        squares = sq_ref[...] + jnp.concatenate(tails, axis=1)
        scale = lax.rsqrt(squares / feature_count + 1e-06)
        vocab_t[...] = (sums * scale).astype(jnp.bfloat16)
        row = lax.broadcasted_iota(jnp.int32, (taps, taps), 0)
        col = lax.broadcasted_iota(jnp.int32, (taps, taps), 1)
        filt = filt_ref[...].astype(jnp.float32)
        for g in range(groups):
            circ = pltpu.roll(
                jnp.broadcast_to(filt[g : g + 1], (taps, taps)), 0, 1, stride=1, stride_axis=0
            )
            toeplitz[g, :taps] = jnp.where(col < row, circ, 0.0).astype(jnp.bfloat16)
            toeplitz[g, taps:] = jnp.where(col >= row, circ, 0.0).astype(jnp.bfloat16)
        cols = taps_ref[...].T
        for i in range(9):
            tap_cols[i] = jnp.broadcast_to(cols[:, i : i + 1], (chans, LANES))
        prod[:, :gsz, :] = jnp.zeros((groups, gsz, taps), jnp.bfloat16)

    for k in range(2):
        carry[k] = jnp.zeros(carry.shape[1:], jnp.float32)

    ids = lax.broadcasted_iota(jnp.int32, (vocab, chunk), 0).astype(jnp.int16)
    one, zero = jnp.ones((), jnp.bfloat16), jnp.zeros((), jnp.bfloat16)
    lane = lax.broadcasted_iota(jnp.int32, (chans, LANES), 1)
    per = chunk // taps
    for n in range(length // chunk):
        toks = jnp.concatenate(
            [tok_ref[n * per + b, pl.ds(genome, 1), :] for b in range(per)], axis=1
        )
        picks = jnp.where(ids == toks.astype(jnp.int16), one, zero)
        proj = jnp.dot(vocab_t[...], picks, preferred_element_type=jnp.float32)
        mixed = []
        for s in range(3):
            cur = proj[s * chans : (s + 1) * chans]
            wide = lambda i: jnp.concatenate([tap_cols[i]] * per, axis=1)
            total = wide(s) * cur
            backs = []
            for k in (1, 2):
                tiles = []
                before = carry[k - 1, s]
                for b in range(per):
                    turned = pltpu.roll(cur[:, b * LANES : (b + 1) * LANES], k, 1)
                    tiles.append(jnp.where(lane < k, before, turned))
                    before = turned
                carry[k - 1, s] = before
                backs.append(jnp.concatenate(tiles, axis=1))
                total = total + wide(3 * k + s) * backs[-1]
            mixed.append(total)
        inner = (mixed[0] * mixed[2]).astype(jnp.bfloat16)
        for b in range(per):
            gate[n * per + b] = mixed[1][:, b * taps : (b + 1) * taps]
            at = (n * per + b + 1) * gsz
            for g in range(groups):
                prod[g, at : at + gsz, :] = inner[g * gsz : (g + 1) * gsz, b * taps : (b + 1) * taps]
    rows = blocks * gsz
    for g in range(groups):
        pair = jnp.concatenate([prod[g, :rows], prod[g, gsz : gsz + rows]], axis=1)
        conv[g] = jnp.dot(pair, toeplitz[g], preferred_element_type=jnp.float32)
    for r in range(blocks):
        b = place_ref[0] ^ r
        at = pl.ds(pl.multiple_of(b * gsz, gsz), gsz)
        filtered = jnp.concatenate([conv[g, at, :] for g in range(groups)], axis=0)
        gated = (gate[b] * filtered).astype(jnp.bfloat16).T
        k, dx, dc = r >> 2, (r >> 1) & 1, r & 1
        if k == 0:
            home[dx, dc, 0] = gated
        elif dx == 1:
            far[k - 1, dc, 0] = gated
        else:
            near[k - 1][dc, 0] = gated


def mixer(place, tokens, own, got, squares, taps_rows, filt, feature_count):
    blocks, genomes, taps = tokens.shape
    vocab, width = own.shape
    chans = width // 3
    groups, _ = filt.shape
    gsz = chans // groups
    hops = blocks // 4
    length = blocks * taps
    whole = lambda *shape: pl.BlockSpec(shape, lambda g, p: (0,) * len(shape))
    near_shape = (2, genomes, taps, chans)
    packs = lambda n: pl.BlockSpec((n, 2, 1, taps, chans), lambda g, p: (0, 0, g, 0, 0))
    return pl.pallas_call(
        functools.partial(mixer_body, feature_count=feature_count, chunk=4 * taps),
        grid_spec=pltpu.PrefetchScalarGridSpec(
            num_scalar_prefetch=1,
            grid=(genomes,),
            in_specs=[
                whole(blocks, genomes, taps),
                whole(vocab, width),
                whole(*got.shape),
                whole(1, vocab),
                whole(*taps_rows.shape),
                whole(groups, taps),
            ],
            out_specs=[packs(2)]
            + [pl.BlockSpec((2, 1, taps, chans), lambda g, p: (0, g, 0, 0))] * (hops - 1)
            + [packs(hops - 1)],
            scratch_shapes=[
                pltpu.VMEM((width, vocab), jnp.bfloat16),
                pltpu.VMEM((groups, 2 * taps, taps), jnp.bfloat16),
                pltpu.VMEM((9, chans, LANES), jnp.float32),
                pltpu.VMEM((2, 3, chans, LANES), jnp.float32),
                pltpu.VMEM((groups, (blocks + 1) * gsz, taps), jnp.bfloat16),
                pltpu.VMEM((blocks, chans, taps), jnp.float32),
                pltpu.VMEM((groups, blocks * gsz, taps), jnp.float32),
            ],
        ),
        out_shape=[jax.ShapeDtypeStruct((2,) + near_shape, jnp.bfloat16)]
        + [jax.ShapeDtypeStruct(near_shape, jnp.bfloat16)] * (hops - 1)
        + [jax.ShapeDtypeStruct((hops - 1,) + near_shape, jnp.bfloat16)],
        compiler_params=pltpu.CompilerParams(vmem_limit_bytes=26 * MIB),
        cost_estimate=pl.CostEstimate(
            flops=2 * genomes * length * vocab * width,
            bytes_accessed=6 * vocab * width + 2 * genomes * length * chans,
            transcendentals=0,
        ),
        name="mixer",
    )(place, tokens, own, got, squares, taps_rows, filt)


def project_body(place_ref, *refs, columns, skip, first, last, tile):
    hops = len(columns)
    mine, other = refs[:hops], refs[hops : 2 * hops]
    cross, cross_other, w_hbm = refs[2 * hops : 2 * hops + 3]
    rest = refs[2 * hops + 3 :]
    if first:
        tok_ref, table_ref, out_ref, gated, slabs, arrivals, picks = rest
    elif last:
        acc_ref, out_ref, gated, slabs, arrivals, ready, leaving = rest
    else:
        acc_ref, out_ref, gated, slabs, arrivals = rest
    chans = cross.shape[-1]
    genomes, rows = cross.shape[1:3]
    wide = 4 * chans
    tiles = w_hbm.shape[0] // tile
    arriving = []
    for t in range(tiles):
        for j, c in enumerate(columns):
            at = pl.multiple_of(((place_ref[0] >> 1) ^ c) * wide, wide)
            copy = pltpu.make_async_copy(
                w_hbm.at[pl.ds(t * tile, tile), pl.ds(at, wide)],
                slabs.at[t, :, pl.ds(j * wide, wide)],
                arrivals.at[t, j],
            )
            copy.start()
            arriving.append(copy)

    core, plane = place_ref[0] & 1, place_ref[1]
    for j in range(hops):
        pieces = (
            (mine[j], 0, core, plane),
            (other[j], 0, core, 1 - plane),
            (cross, j, 1 - core, plane),
            (cross_other, skip + j, 1 - core, 1 - plane),
        )
        for ref, lead, from_core, from_plane in pieces:
            at = j * wide + (2 * from_core + from_plane) * chans
            lanes = pl.ds(pl.multiple_of(at, LANES), chans)
            for g in range(genomes):
                gated[g * rows : (g + 1) * rows, lanes] = ref[lead, g]
    if first:
        vocab = table_ref.shape[0]
        toks = tok_ref[place_ref[0]]
        toks = jnp.concatenate([toks[g : g + 1] for g in range(genomes)], axis=1)
        ids = lax.broadcasted_iota(jnp.int32, (vocab, genomes * rows), 0)
        picks[...] = jnp.where(ids == toks, 1.0, 0.0).T.astype(jnp.bfloat16)

    sending = []
    for t in range(tiles):
        at = slice(t * tile, (t + 1) * tile)
        for j in range(hops):
            arriving[t * hops + j].wait()
        total = lax.dot_general(
            gated[...], slabs[t], (((1,), (1,)), ((), ())), preferred_element_type=jnp.float32
        )
        if first:
            total = total + jnp.dot(
                picks[...], table_ref[:, at], preferred_element_type=jnp.float32
            )
        for g in range(genomes):
            part = total[g * rows : (g + 1) * rows]
            if not first:
                part = part + acc_ref[g, :, at]
            if last:
                ready[g, :, at] = part.astype(ready.dtype)
            else:
                out_ref[g, :, at] = part
        if last:
            copy = pltpu.make_async_copy(ready.at[:, :, at], out_ref.at[:, :, at], leaving.at[t])
            copy.start()
            sending.append(copy)
    for copy in sending:
        copy.wait()


def project(place, mine, other, cross, columns, w_out, start, last=False):
    hops = len(mine)
    first = isinstance(start, tuple)
    cross, cross_other = cross if isinstance(cross, tuple) else (cross, cross)
    skip = cross_other.shape[0] - hops
    _, genomes, rows, chans = cross.shape
    feats = w_out.shape[0]
    tile = 1024
    tiles = feats // tile
    vmem = pl.BlockSpec(memory_space=pltpu.VMEM)
    anywhere = pl.BlockSpec(memory_space=pl.ANY)
    operands = mine + other + [cross, cross_other, w_out]
    in_specs = [pl.BlockSpec(memory_space=pltpu.SMEM)] + [vmem] * (2 * hops + 2) + [anywhere]
    scratch = [
        pltpu.VMEM((genomes * rows, hops * 4 * chans), jnp.bfloat16),
        pltpu.VMEM((tiles, tile, hops * 4 * chans), jnp.bfloat16),
        pltpu.SemaphoreType.DMA((tiles, hops)),
    ]
    if first:
        operands += list(start)
        in_specs += [vmem, vmem]
        scratch.append(pltpu.VMEM((genomes * rows, start[1].shape[0]), jnp.bfloat16))
    else:
        operands.append(start)
        in_specs.append(vmem)
    shape = (genomes, rows, feats)
    if last:
        scratch += [pltpu.VMEM(shape, jnp.bfloat16), pltpu.SemaphoreType.DMA((tiles,))]
    return pl.pallas_call(
        functools.partial(
            project_body, columns=columns, skip=skip, first=first, last=last, tile=tile
        ),
        in_specs=in_specs,
        out_specs=anywhere if last else vmem,
        scratch_shapes=scratch,
        out_shape=jax.ShapeDtypeStruct(shape, jnp.bfloat16 if last else jnp.float32),
        compiler_params=pltpu.CompilerParams(vmem_limit_bytes=40 * MIB),
        cost_estimate=pl.CostEstimate(
            flops=2 * genomes * rows * feats * hops * 4 * chans,
            bytes_accessed=2 * feats * hops * 4 * chans + 6 * genomes * rows * feats,
            transcendentals=0,
        ),
        name="project",
    )(place, *operands)


def swap_wt(shard):
    return lax.ppermute(shard, "wt", [(0, 1), (1, 0)])


def swap_seq(shard, step):
    return lax.ppermute(shard, "seq", [(i, i ^ step) for i in range(lax.axis_size("seq"))])


def swap_core(mine, other):
    return swap_seq(jnp.stack([a[1] for a in mine + other]), 1)


def shared_block(tokens, embed_table, norm_gain, w_in, short_taps, filters, w_out):
    me = lax.axis_index("wt")
    local_chans = w_in.shape[2]
    chans = local_chans // 2
    groups = filters.shape[0] // 2
    feature_count = embed_table.shape[1] * lax.axis_size("wt")
    w_streams = jnp.transpose(w_in, (1, 0, 2))
    place = jnp.stack([lax.axis_index("seq"), me]).astype(jnp.int32)
    pick = lambda which: jnp.reshape(which, (1,)).astype(jnp.int32)
    seqs, planes = lax.axis_size("seq"), lax.axis_size("wt")
    sent, squares, copies = vocab_share(
        pick(1 - me), embed_table, norm_gain, w_streams, jnp.bfloat16, tokens, seqs * planes
    )
    got = swap_wt(sent)
    all_tokens = lax.all_to_all(copies, ("seq", "wt"), 0, 0, tiled=True)
    all_tokens = all_tokens.reshape(seqs, planes, tokens.shape[1])
    (own,) = vocab_share(pick(me), embed_table, norm_gain, w_streams, jnp.float32)
    taps_rows = lax.dynamic_slice_in_dim(
        short_taps.astype(jnp.float32).reshape(9, local_chans), me * chans, chans, 1
    )
    taps_rows = jnp.pad(taps_rows, ((0, 7), (0, 0)))
    filt = lax.dynamic_slice_in_dim(filters, me * groups, groups, 0)
    home, *near, far = mixer(
        place, all_tokens, own, got, squares, taps_rows, filt, feature_count
    )
    hops = len(near) + 1
    order = sorted(range(1, hops), key=lambda k: (k == 1, k))
    bar = lax.optimization_barrier
    arrived = swap_seq(far, 2)
    home_other = swap_wt(home)
    near_mine = {k: swap_seq(near[k - 1], 4 * k) for k in order}
    arrived, near_mine[1] = bar((arrived, near_mine[1]))
    far_mine = {k: swap_seq(arrived[k - 1], 4 * k) for k in order}
    crossed = swap_seq(jnp.stack([home[1], home_other[1]]), 2)
    first_mine, first_other = [home[0]], [home_other[0]]
    cross = swap_core(first_mine, first_other)
    total = project(
        place, first_mine, first_other, cross, [0], w_out, (all_tokens, embed_table)
    )
    near_mine = [near_mine[k] for k in range(1, hops)]
    near_other = swap_wt(jnp.stack(near_mine))
    near_mine = [crossed[0]] + near_mine
    near_other = [crossed[1]] + [near_other[k] for k in range(hops - 1)]
    cross = swap_core(near_mine, near_other)
    far_mine = [far_mine[k] for k in range(1, hops)]
    far_mine, cross = bar((far_mine, cross))
    far_other = swap_wt(jnp.stack(far_mine))
    far_cross = swap_seq(jnp.stack([a[1] for a in far_mine]), 1)
    columns = [1] + [2 * k for k in range(1, hops)]
    total, _ = bar((total, far_mine))
    total = project(place, near_mine, near_other, cross, columns, w_out, total)
    far_other, total = bar((far_other, total))
    far_other = [far_other[k] for k in range(hops - 1)]
    cross = (far_cross, swap_seq(jnp.stack([a[1] for a in far_other]), 1))
    columns = [2 * k + 1 for k in range(1, hops)]
    return project(place, far_mine, far_other, cross, columns, w_out, total, True)


def local(*args):
    tokens, embed_table, norm_gain, w_in, short_taps, filters, w_out = args
    ranks = lax.axis_size("seq")
    wide = lax.axis_size("wt") == 2 and w_in.shape[2] == 2 * LANES and ranks in (8, 16, 32)
    aligned = tokens.shape[1] == filters.shape[1] == LANES and w_out.shape[0] % 1024 == 0
    if wide and aligned and tokens.shape[0] == 1:
        return shared_block(*args)
    return plain_block(*args)


def solution(mesh):
    placed = (
        P("wt", "seq"),
        P(None, "wt"),
        P("wt"),
        P("wt", None, "seq"),
        P(None, None, "seq"),
        P("seq", None),
        P("wt", None),
    )
    return jax.shard_map(
        local, mesh=mesh, in_specs=placed, out_specs=P(None, "seq", "wt"), check_vma=False
    )
```
